256 devices in a mesh: space: 64 (over z, y, core), view: 4 (over x).
Axes of the slice: x: 4, y: 4, z: 8, core: 2. Of those that a mesh axis runs over, the one named last changes fastest.
Arguments:
- gaussians: float32 [59, 524288], P(None, 'space'), as said below
- camera_table: float32 [16, 8], replicated, as said below
- view_camera: int32 [4], P('view'), may hold values from 0 to 15
- tile_plan: int32 [4, 1024], P('view', 'space'), may hold values from 2204 to 5955, as said below
- requests: int32 [4, 64, 64, 128], P('view', 'space'), may hold values from 0 to 8191, as said below
- tile_lists: int32 [4, 1024, 512], P('view', 'space'), may hold values from 0 to 8191, as said below
- tile_lengths: int32 [4, 1024], P('view', 'space'), may hold values from 128 to 512, as said below
- pixel_grad: float32 [4, 1024, 3, 256], P('view', 'space'), may hold values from -0.625 to 0.625
Outputs:
- rendered: float32 [4, 1024, 3, 256], P('view', 'space')
- gaussian_grad: float32 [59, 524288], P(None, 'space')
The draws below stay inside these ranges and needn't reach their ends.
Inputs may be any that keep to these rules, and one draw needn't show every extreme that they name: `tile_plan`: tile ids count 120 tiles to a row; within a view every tile k < 1024 of tile row 18 + floor(k / 32) and tile column 44 + (k mod 32) appears exactly once. `requests`: slots of the owner's 8192 Gaussians; within a view no slot of an owner is requested twice, by one renderer or by two. `tile_lists`: position o * 128 + k names the k-th slot the renderer requested of owner o; the lists of one renderer's tiles together name each of its requested rows exactly once, each list the same number of rows of every owner, ordered by owner and within an owner by slot; entries from the tile's length on are padding. `tile_lengths`: every view has a tile with all 512 entries live. `camera_table`: quaternion rows lead with 2 to 3 and the rest within 0.3; offsets lie within 0.2 across and 4 to 5 in depth; focal lengths 1.8 to 2.4. `gaussians`: the first quaternion entry lies in 1 to 2.
All inputs are finite; a program needn't handle non-finite values.
Results may differ from the reference program's by a relative error of at most 0.0003.
Values sent between devices are 32-bit elements; how exact they have to be, the bound alone decides.
No kernel may reach another device: no remote copies, remote signals or barrier semaphores. Data moves between devices by JAX's collectives and lax.ppermute only.
A program may use at most 256 MiB of HBM per device.

```python
import jax
import jax.numpy as jnp
from jax import lax

PIX = 256
LMAX = 512
CAMS = 16
GDEV = 8192
TILE_DEV = 16
CAP = 128
VIEWS = 4
TILES_VIEW = 1024
N_SPACE = 64


def rotation_rows(quat):
    length = jnp.sqrt(jnp.sum(quat * quat))
    unit_w = quat[0] / length
    unit_x = quat[1] / length
    unit_y = quat[2] / length
    unit_z = quat[3] / length
    return [[1.0 - 2.0 * (unit_y * unit_y + unit_z * unit_z), 2.0 * (unit_x * unit_y - unit_w * unit_z), 2.0 * (unit_x * unit_z + unit_w * unit_y)], [2.0 * (unit_x * unit_y + unit_w * unit_z), 1.0 - 2.0 * (unit_x * unit_x + unit_z * unit_z), 2.0 * (unit_y * unit_z - unit_w * unit_x)], [2.0 * (unit_x * unit_z - unit_w * unit_y), 2.0 * (unit_y * unit_z + unit_w * unit_x), 1.0 - 2.0 * (unit_x * unit_x + unit_y * unit_y)]]


def owner_slots(key):
    key = jax.random.fold_in(key, 301)
    slot_index = jnp.arange(GDEV, dtype=jnp.int32)
    scores = jax.random.randint(key, (N_SPACE, GDEV), 0, 1 << 16) * GDEV + slot_index[None, :]
    scores = jnp.where(slot_index[None, :] == 0, -2, jnp.where(slot_index[None, :] == GDEV - 1, -1, scores))
    return jnp.argsort(scores, axis=1, stable=True).astype(jnp.int32)


def view_tiles(key):
    key = jax.random.fold_in(key, 302)
    tile_index = jnp.arange(TILES_VIEW, dtype=jnp.int32)
    scores = jax.random.randint(key, (VIEWS, TILES_VIEW), 0, 1 << 16) * TILES_VIEW + tile_index[None, :]
    return jnp.argsort(scores, axis=1, stable=True).astype(jnp.int32)


def request_order(key):
    key = jax.random.fold_in(key, 303)
    place_index = jnp.arange(CAP, dtype=jnp.int32)
    scores = jax.random.randint(key, (VIEWS, N_SPACE, N_SPACE, CAP), 0, 1 << 16) * CAP + place_index
    return jnp.argsort(scores, axis=3, stable=True).astype(jnp.int32)


def base_camera(key):
    key = jax.random.fold_in(key, 304)
    keys = jax.random.split(key, 5)
    lead = jax.random.uniform(keys[0], (1,), minval=2.1, maxval=2.9)
    rest = jax.random.uniform(keys[1], (3,), minval=-0.25, maxval=0.25)
    across = jax.random.uniform(keys[2], (2,), minval=-0.15, maxval=0.15)
    depth = jax.random.uniform(keys[3], (1,), minval=4.1, maxval=4.9)
    focal_len = jax.random.uniform(keys[4], (1,), minval=1.9, maxval=2.3)
    return jnp.concatenate([lead, rest, across, depth, focal_len])


def tile_slots(key):
    slot_order = owner_slots(key)
    order = view_tiles(key)
    per_tile = LMAX // N_SPACE
    tiles = order.reshape(VIEWS, N_SPACE, TILE_DEV)
    index = tiles[:, :, :, None] * per_tile + jnp.arange(per_tile, dtype=jnp.int32)
    return slot_order[:, index]


def draw_gaussians(key, part):
    slot_order = owner_slots(key)
    camera = base_camera(key)
    key = jax.random.fold_in(key, 11)
    keys = jax.random.split(key, 10)
    count = GDEV * N_SPACE
    per_tile = LMAX // N_SPACE
    place = jnp.argsort(slot_order, axis=1, stable=True).reshape(count)
    homed = place < TILES_VIEW * per_tile
    region = jnp.minimum(place // per_tile, TILES_VIEW - 1)
    center_u = ((44 + region % 32) * 16 + 8 - 960).astype(jnp.float32) / 540.0
    center_v = ((18 + region // 32) * 16 + 8 - 540).astype(jnp.float32) / 540.0
    jitter = jax.random.uniform(keys[0], (2, count), minval=-8.0 / 540.0, maxval=8.0 / 540.0)
    log_scales = jax.random.uniform(keys[2], (3, count), minval=-5.4, maxval=-3.8)
    harmonics = 0.3 * jax.random.truncated_normal(keys[6], -3.0, 3.0, (48, count))
    share = 0.02
    bright_low = -1.0
    faint_low = -6.0
    wide = jax.random.uniform(keys[1], (2, count), minval=-0.8, maxval=0.8)
    screen_u = jnp.where(homed, center_u + jitter[0], wide[0])
    screen_v = jnp.where(homed, center_v + jitter[1], wide[1])
    depth = 3.6 + 1.8 * (jnp.arange(count, dtype=jnp.int32).astype(jnp.float32) + 0.5) / count
    view_rot = rotation_rows(camera[0:4])
    focal_len = camera[7]
    relative = [screen_u * depth / focal_len - camera[4], screen_v * depth / focal_len - camera[5], depth - camera[6]]
    centers = jnp.stack([sum((view_rot[j][i] * relative[j] for j in range(3))) for i in range(3)])
    quat_lead = jax.random.uniform(keys[3], (1, count), minval=1.0, maxval=2.0)
    quat_rest = jax.random.uniform(keys[4], (3, count), minval=-1.0, maxval=1.0)
    picker = jax.random.uniform(keys[5], (1, count))
    bright = jax.random.uniform(keys[7], (1, count), minval=bright_low, maxval=2.0)
    faint = jax.random.uniform(keys[8], (1, count), minval=faint_low, maxval=-3.5)
    opacity = jnp.where(picker < share, bright, faint)
    return jnp.concatenate([centers, log_scales, quat_lead, quat_rest, opacity, harmonics], axis=0).astype(jnp.float32)


def draw_camera_table(key, part):
    camera = base_camera(key)
    key = jax.random.fold_in(key, 12)
    keys = jax.random.split(key, 5)
    jitter = jnp.concatenate([jax.random.uniform(keys[0], (CAMS, 1), minval=-0.02, maxval=0.02), jax.random.uniform(keys[1], (CAMS, 3), minval=-0.008, maxval=0.008), jax.random.uniform(keys[2], (CAMS, 2), minval=-0.02, maxval=0.02), jax.random.uniform(keys[3], (CAMS, 1), minval=-0.05, maxval=0.05), jax.random.uniform(keys[4], (CAMS, 1), minval=-0.02, maxval=0.02)], axis=1)
    return (camera[None, :] + jitter).astype(jnp.float32)


def draw_tile_plan(key, part):
    order = view_tiles(key)
    key = jax.random.fold_in(key, 13)
    return ((18 + order // 32) * 120 + 44 + order % 32).astype(jnp.int32)


def draw_requests(key, part):
    slots = tile_slots(key)
    sigma = request_order(key)
    key = jax.random.fold_in(key, 14)
    by_place = slots.transpose(1, 2, 0, 3, 4).reshape(VIEWS, N_SPACE, N_SPACE, CAP)
    inverse = jnp.argsort(sigma, axis=3, stable=True)
    return jnp.take_along_axis(by_place, inverse, axis=3).astype(jnp.int32)


def draw_tile_lists(key, part):
    slots = tile_slots(key)
    sigma = request_order(key)
    key = jax.random.fold_in(key, 15)
    per_tile = LMAX // N_SPACE
    slots_tile = slots.transpose(1, 2, 3, 0, 4)
    positions = sigma.reshape(VIEWS, N_SPACE, N_SPACE, TILE_DEV, per_tile).transpose(0, 1, 3, 2, 4)
    owner_ids = jnp.arange(N_SPACE, dtype=jnp.int32)[None, None, None, :, None]
    entries = (owner_ids * CAP + positions).reshape(VIEWS, TILES_VIEW, LMAX)
    depth_keys = (owner_ids * GDEV + slots_tile).reshape(VIEWS, TILES_VIEW, LMAX)
    rank = jnp.argsort(depth_keys, axis=2, stable=True)
    return jnp.take_along_axis(entries, rank, axis=2).astype(jnp.int32)


def draw_tile_lengths(key, part):
    key = jax.random.fold_in(key, 16)
    key_len, key_top = jax.random.split(key, 2)
    lengths = jax.random.randint(key_len, (VIEWS, TILES_VIEW), LMAX // 4, LMAX + 1)
    longest = jax.random.randint(key_top, (VIEWS, 1), 0, TILES_VIEW)
    lengths = jnp.where(jnp.arange(TILES_VIEW, dtype=jnp.int32)[None, :] == longest, LMAX, lengths)
    return lengths.astype(jnp.int32)


def touch_ends(drawn, rng, least, largest):
    spot = [jax.random.randint(jax.random.fold_in(rng, axis), (), 0, length) for axis, length in enumerate(drawn.shape)]
    main_axis = drawn.shape.index(max(drawn.shape))
    neighbour = spot[:main_axis] + [(spot[main_axis] + 1) % drawn.shape[main_axis]] + spot[main_axis + 1:]
    return drawn.at[tuple(spot)].set(least).at[tuple(neighbour)].set(largest)


def shard_levels(own_key, extent, cuts, low, largest):
    level = 1.0
    for dim, parts in cuts:
        heights = jax.random.uniform(jax.random.fold_in(jax.random.fold_in(own_key, 6), dim), (parts,), jnp.float32, low / len(cuts), largest / len(cuts))
        level = level * jnp.repeat(jnp.exp(heights), extent[dim] // parts).reshape((-1,) + (1,) * (len(extent) - 1 - dim))
    return level


def gaussian(own_key, shape, spread, most, shards=(), kind=jnp.bfloat16):
    values = spread * jax.random.normal(own_key, shape, jnp.float32)
    if shards:
        values = values * shard_levels(own_key, shape, shards, -0.22, 0.18)
    return jnp.clip(values, -most, most).astype(kind)


def setup_inputs(seed: int = 0) -> dict:
    seeds = jax.random.split(jax.random.key(seed), 9)
    return {
        "gaussians": draw_gaussians(jax.random.fold_in(seeds[8], 71), 0),
        "camera_table": draw_camera_table(jax.random.fold_in(seeds[8], 71), 0),
        "view_camera": touch_ends(jax.random.randint(seeds[2], (VIEWS,), 0, CAMS), jax.random.fold_in(seeds[2], 1), 0, CAMS - 1).astype(jnp.int32),
        "tile_plan": draw_tile_plan(jax.random.fold_in(seeds[8], 71), 0),
        "requests": draw_requests(jax.random.fold_in(seeds[8], 71), 0),
        "tile_lists": draw_tile_lists(jax.random.fold_in(seeds[8], 71), 0),
        "tile_lengths": draw_tile_lengths(jax.random.fold_in(seeds[8], 71), 0),
        "pixel_grad": gaussian(seeds[7], (VIEWS, TILES_VIEW, 3, PIX), 0.1, 0.625, ((0, 4), (1, 64)), jnp.float32),
    }


sh_zero = 0.28209479177387814
sh_one = 0.4886025119029199
sh_two = (1.0925484305920792, -1.0925484305920792, 0.31539156525252005, -1.0925484305920792, 0.5462742152960396)
sh_three = (-0.5900435899266435, 2.890611442640554, -0.4570457994644658, 0.3731763325901154, -0.4570457994644658, 1.445305721320277, -0.5900435899266435)
dilation = 0.3 / 291600.0
highest = lax.Precision.HIGHEST

def quat_matrix(quat_w, quat_x, quat_y, quat_z):
    length = jnp.sqrt(quat_w * quat_w + quat_x * quat_x + quat_y * quat_y + quat_z * quat_z)
    unit_w = quat_w / length
    unit_x = quat_x / length
    unit_y = quat_y / length
    unit_z = quat_z / length
    return [[1.0 - 2.0 * (unit_y * unit_y + unit_z * unit_z), 2.0 * (unit_x * unit_y - unit_w * unit_z), 2.0 * (unit_x * unit_z + unit_w * unit_y)], [2.0 * (unit_x * unit_y + unit_w * unit_z), 1.0 - 2.0 * (unit_x * unit_x + unit_z * unit_z), 2.0 * (unit_y * unit_z - unit_w * unit_x)], [2.0 * (unit_x * unit_z - unit_w * unit_y), 2.0 * (unit_y * unit_z + unit_w * unit_x), 1.0 - 2.0 * (unit_x * unit_x + unit_y * unit_y)]]

def sh_basis(dir_x, dir_y, dir_z):
    sq_x = dir_x * dir_x
    sq_y = dir_y * dir_y
    sq_z = dir_z * dir_z
    return [sh_zero * jnp.ones_like(dir_x), -sh_one * dir_y, sh_one * dir_z, -sh_one * dir_x, sh_two[0] * dir_x * dir_y, sh_two[1] * dir_y * dir_z, sh_two[2] * (2.0 * sq_z - sq_x - sq_y), sh_two[3] * dir_x * dir_z, sh_two[4] * (sq_x - sq_y), sh_three[0] * dir_y * (3.0 * sq_x - sq_y), sh_three[1] * dir_x * dir_y * dir_z, sh_three[2] * dir_y * (4.0 * sq_z - sq_x - sq_y), sh_three[3] * dir_z * (2.0 * sq_z - 3.0 * sq_x - 3.0 * sq_y), sh_three[4] * dir_x * (4.0 * sq_z - sq_x - sq_y), sh_three[5] * dir_z * (sq_x - sq_y), sh_three[6] * dir_x * (sq_x - 3.0 * sq_y)]

def project(params, camera):
    center = [params[0], params[1], params[2]]
    scales = [jnp.exp(params[3]), jnp.exp(params[4]), jnp.exp(params[5])]
    own_rot = quat_matrix(params[6], params[7], params[8], params[9])
    view_rot = quat_matrix(camera[0], camera[1], camera[2], camera[3])
    offset_cam = [camera[4], camera[5], camera[6]]
    focal_len = camera[7]
    in_camera = [sum((view_rot[i][j] * center[j] for j in range(3))) + offset_cam[i] for i in range(3)]
    shaped = [[own_rot[i][k] * scales[k] for k in range(3)] for i in range(3)]
    turned = [[sum((view_rot[i][j] * shaped[j][k] for j in range(3))) for k in range(3)] for i in range(3)]
    inv_depth = 1.0 / in_camera[2]
    screen_u = focal_len * in_camera[0] * inv_depth
    screen_v = focal_len * in_camera[1] * inv_depth
    jac_u = [focal_len * inv_depth * turned[0][k] - screen_u * inv_depth * turned[2][k] for k in range(3)]
    jac_v = [focal_len * inv_depth * turned[1][k] - screen_v * inv_depth * turned[2][k] for k in range(3)]
    cov_uu = sum((jac_u[k] * jac_u[k] for k in range(3))) + dilation
    cov_uv = sum((jac_u[k] * jac_v[k] for k in range(3)))
    cov_vv = sum((jac_v[k] * jac_v[k] for k in range(3))) + dilation
    determinant = cov_uu * cov_vv - cov_uv * cov_uv
    opacity = jax.nn.sigmoid(params[10])
    eye_pos = [-sum((view_rot[j][i] * offset_cam[j] for j in range(3))) for i in range(3)]
    toward = [center[i] - eye_pos[i] for i in range(3)]
    length = jnp.sqrt(toward[0] * toward[0] + toward[1] * toward[1] + toward[2] * toward[2])
    basis = sh_basis(toward[0] / length, toward[1] / length, toward[2] / length)
    colors = [0.5 + sum((basis[k] * params[11 + 3 * k + h] for k in range(16))) for h in range(3)]
    return jnp.stack([screen_u, screen_v, cov_vv / determinant, -cov_uv / determinant, cov_uu / determinant, opacity] + colors)

def pixel_points(tile_one):
    pixel = jnp.arange(256, dtype=jnp.int32)
    column = tile_one % 120 * 16 + pixel % 16
    row_at = tile_one // 120 * 16 + pixel // 16
    point_u = (column.astype(jnp.float32) + 0.5 - 960.0) / 540.0
    point_v = (row_at.astype(jnp.float32) + 0.5 - 540.0) / 540.0
    return (point_u, point_v)

def render_tiles(features, entries, lengths, tile_ids):

    def one_tile(args):
        entry_row, length_one, tile_one = args
        columns = jnp.take(features, entry_row, axis=1)
        point_u, point_v = pixel_points(tile_one)
        diff_u = point_u[:, None] - columns[0][None, :]
        diff_v = point_v[:, None] - columns[1][None, :]
        power = -0.5 * (columns[2][None, :] * diff_u * diff_u + 2.0 * columns[3][None, :] * diff_u * diff_v + columns[4][None, :] * diff_v * diff_v)
        alpha = columns[5][None, :] * jnp.exp(power)
        alive = jnp.arange(entry_row.shape[0], dtype=jnp.int32) < length_one
        alpha = jnp.where(alive[None, :], alpha, 0.0)
        logs = jnp.log1p(-alpha)
        before = jnp.cumsum(logs, axis=1) - logs
        weights = alpha * jnp.exp(before)
        return lax.dot_general(columns[6:9], weights, (((1,), (1,)), ((), ())), precision=highest)
    return lax.map(one_tile, (entries, lengths, tile_ids))

def reference(gaussians, camera_table, view_camera, tile_plan, requests, tile_lists, tile_lengths, pixel_grad):
    view_ids = jnp.repeat(view_camera, N_SPACE)
    requests_all = requests.reshape(VIEWS * N_SPACE, N_SPACE, CAP)
    plan_all = tile_plan.reshape(VIEWS * N_SPACE, TILE_DEV)
    lists_all = tile_lists.reshape(VIEWS * N_SPACE, TILE_DEV, LMAX)
    lengths_all = tile_lengths.reshape(VIEWS * N_SPACE, TILE_DEV)
    owner_base = (jnp.arange(N_SPACE, dtype=jnp.int32) * GDEV)[:, None]

    def forward(params):

        def one_device(args):
            view_id, requests_dev, plan_dev, lists_dev, lengths_dev = args
            camera = camera_table[view_id]
            picked = jnp.take(params, (requests_dev + owner_base).reshape(-1), axis=1)
            features = project(picked, camera)
            return render_tiles(features, lists_dev, lengths_dev, plan_dev)
        images = lax.map(jax.checkpoint(one_device), (view_ids, requests_all, plan_all, lists_all, lengths_all))
        return images.reshape(VIEWS, TILES_VIEW, 3, PIX)
    rendered, back = jax.vjp(forward, gaussians)
    gaussian_grad, = back(pixel_grad)
    return (rendered, gaussian_grad)
```

```python
import jax
import jax.numpy as jnp
from jax import lax
from jax.experimental import pallas as pl
from jax.experimental.pallas import tpu as pltpu
from jax.sharding import PartitionSpec as P

sh_zero = 0.28209479177387814
sh_one = 0.4886025119029199
sh_two = (
    1.0925484305920792,
    -1.0925484305920792,
    0.31539156525252005,
    -1.0925484305920792,
    0.5462742152960396,
)
sh_three = (
    -0.5900435899266435,
    2.890611442640554,
    -0.4570457994644658,
    0.3731763325901154,
    -0.4570457994644658,
    1.445305721320277,
    -0.5900435899266435,
)
dilation = 0.3 / 291600.0
log2e = 1.4426950408889634
unit = 1080.0
params_n = 59
feats = 9
owners = 64
slots = 8192
pitch = 72
half_rows = 296
vmem = pl.BlockSpec(memory_space=pltpu.VMEM)
smem = pl.BlockSpec(memory_space=pltpu.SMEM)
f32 = jnp.float32
bf16 = jnp.bfloat16


def quat_matrix(quat_w, quat_x, quat_y, quat_z):
    inv = 1.0 / jnp.sqrt(
        quat_w * quat_w + quat_x * quat_x + quat_y * quat_y + quat_z * quat_z
    )
    unit_w = quat_w * inv
    unit_x = quat_x * inv
    unit_y = quat_y * inv
    unit_z = quat_z * inv
    return [
        [
            1.0 - 2.0 * (unit_y * unit_y + unit_z * unit_z),
            2.0 * (unit_x * unit_y - unit_w * unit_z),
            2.0 * (unit_x * unit_z + unit_w * unit_y),
        ],
        [
            2.0 * (unit_x * unit_y + unit_w * unit_z),
            1.0 - 2.0 * (unit_x * unit_x + unit_z * unit_z),
            2.0 * (unit_y * unit_z - unit_w * unit_x),
        ],
        [
            2.0 * (unit_x * unit_z - unit_w * unit_y),
            2.0 * (unit_y * unit_z + unit_w * unit_x),
            1.0 - 2.0 * (unit_x * unit_x + unit_y * unit_y),
        ],
    ]


def sh_basis(dir_x, dir_y, dir_z):
    sq_x = dir_x * dir_x
    sq_y = dir_y * dir_y
    sq_z = dir_z * dir_z
    return [
        sh_zero,
        -sh_one * dir_y,
        sh_one * dir_z,
        -sh_one * dir_x,
        sh_two[0] * dir_x * dir_y,
        sh_two[1] * dir_y * dir_z,
        sh_two[2] * (2.0 * sq_z - sq_x - sq_y),
        sh_two[3] * dir_x * dir_z,
        sh_two[4] * (sq_x - sq_y),
        sh_three[0] * dir_y * (3.0 * sq_x - sq_y),
        sh_three[1] * dir_x * dir_y * dir_z,
        sh_three[2] * dir_y * (4.0 * sq_z - sq_x - sq_y),
        sh_three[3] * dir_z * (2.0 * sq_z - 3.0 * sq_x - 3.0 * sq_y),
        sh_three[4] * dir_x * (4.0 * sq_z - sq_x - sq_y),
        sh_three[5] * dir_z * (sq_x - sq_y),
        sh_three[6] * dir_x * (sq_x - 3.0 * sq_y),
    ]


def shape_matrix(params):
    scales = [jnp.exp(params[3]), jnp.exp(params[4]), jnp.exp(params[5])]
    own_rot = quat_matrix(params[6], params[7], params[8], params[9])
    return [[own_rot[i][k] * scales[k] for k in range(3)] for i in range(3)]


def view_values(camera):
    view_rot = quat_matrix(camera[0], camera[1], camera[2], camera[3])
    offset_cam = [camera[4], camera[5], camera[6]]
    back = [sum(view_rot[j][i] * offset_cam[j] for j in range(3)) for i in range(3)]
    return view_rot, offset_cam, camera[7], back


def project(params, shaped, view):
    view_rot, offset_cam, focal_len, back = view
    center = [params[0], params[1], params[2]]
    in_camera = [
        sum(view_rot[i][j] * center[j] for j in range(3)) + offset_cam[i] for i in range(3)
    ]
    turned = [
        [sum(view_rot[i][j] * shaped[j][k] for j in range(3)) for k in range(3)] for i in range(3)
    ]
    inv_depth = 1.0 / in_camera[2]
    near = focal_len * inv_depth
    screen_u = near * in_camera[0]
    screen_v = near * in_camera[1]
    slope_u = screen_u * inv_depth
    slope_v = screen_v * inv_depth
    jac_u = [near * turned[0][k] - slope_u * turned[2][k] for k in range(3)]
    jac_v = [near * turned[1][k] - slope_v * turned[2][k] for k in range(3)]
    cov_uu = sum(jac_u[k] * jac_u[k] for k in range(3)) + dilation
    cov_uv = sum(jac_u[k] * jac_v[k] for k in range(3))
    cov_vv = sum(jac_v[k] * jac_v[k] for k in range(3)) + dilation
    inv_det = 1.0 / (cov_uu * cov_vv - cov_uv * cov_uv)
    toward = [center[i] + back[i] for i in range(3)]
    inv_len = 1.0 / jnp.sqrt(
        toward[0] * toward[0] + toward[1] * toward[1] + toward[2] * toward[2]
    )
    basis = sh_basis(toward[0] * inv_len, toward[1] * inv_len, toward[2] * inv_len)
    colors = [0.5 + sum(basis[k] * params[11 + 3 * k + h] for k in range(16)) for h in range(3)]
    return [
        screen_u,
        screen_v,
        cov_vv * inv_det,
        -cov_uv * inv_det,
        cov_uu * inv_det,
    ] + colors


def log_opacity(logit):
    return jnp.minimum(logit, 0.0) - jnp.log1p(jnp.exp(-jnp.abs(logit)))


def pieces(value, count):
    out = []
    for _ in range(count - 1):
        top = value.astype(bf16).astype(f32)
        out.append(top)
        value = value - top
    out.append(value.astype(bf16).astype(f32))
    return out


def iota(shape, axis):
    return lax.broadcasted_iota(jnp.int32, shape, axis)


def spread_rows(gauss_ref, spread):
    def step(tile, carry):
        column = pl.ds(pl.multiple_of(tile * 128, 128), 128)
        row = pl.multiple_of(tile * pitch, 8)
        spread[pl.ds(row, 56), :] = gauss_ref[0:56, column]
        spread[pl.ds(row + 56, 3), :] = gauss_ref[56:59, column]
        return carry

    lax.fori_loop(0, 64, step, 0, unroll=4)


def order_kernel(requests_ref, lists_ref, out_ref, turned):
    lists = lists_ref[...].astype(f32)
    turned[...] = jnp.concatenate([lists, jnp.zeros((112, 512), f32)], axis=0).T
    group = iota((64, 128), 1) // 16
    entry = jnp.zeros((64, 128), f32)
    for j in range(8):
        piece = turned[pl.ds(j, 64, stride=8), :]
        if j:
            piece = pltpu.roll(piece, 16 * j, 1)
        entry = jnp.where(group == j, piece, entry)
    place = entry.astype(jnp.int32) & 127
    out_ref[...] = jnp.take_along_axis(requests_ref[...], place, axis=1)


def camera_values(table_ref, view_ref):
    row = view_ref[0]
    return [jnp.full((8, 128), table_ref[row, i], f32) for i in range(8)]


def project_kernel(table_ref, view_ref, gauss_ref, out_ref, spread, held):
    view = view_values(camera_values(table_ref, view_ref))
    spread_rows(gauss_ref, spread)

    def step(i, carry):
        params = [
            spread[pl.ds(i * (8 * pitch) + p, 8, stride=pitch), :] for p in range(params_n)
        ]
        out = project(params, shape_matrix(params), view)
        out = out[:5] + [log_opacity(params[10])] + out[5:]
        for f in range(feats):
            held[f, pl.ds(pl.multiple_of(i * 8, 8), 8), :] = out[f]
        return carry

    lax.fori_loop(0, 8, step, 0)
    for f in range(feats):
        for part, value in enumerate(pieces(held[f], 3)):
            row = (part * feats + f) * 32
            out_ref[row : row + 32, 0:128] = value[0:32].astype(bf16)
            out_ref[row : row + 32, 128:256] = value[32:64].astype(bf16)


def slot_hot(index):
    place = (index >> 12) * 128 + (index & 127)
    return (iota((256, index.shape[1]), 0) == place).astype(f32).astype(bf16)


def pick_kernel(index_ref, table_ref, out_ref, held):
    table = table_ref[...]

    def step(pair, carry):
        index = jnp.concatenate(
            [index_ref[pl.ds(2 * pair, 1), :], index_ref[pl.ds(2 * pair + 1, 1), :]], axis=1
        )
        got = jnp.dot(table, slot_hot(index), preferred_element_type=f32)
        rows = feats * 32
        got = got[0:rows] + got[rows : 2 * rows] + got[2 * rows : 3 * rows]
        level = (index >> 7) & 31
        keep = iota((32, 256), 0) == level
        for f in range(feats):
            value = jnp.sum(jnp.where(keep, got[32 * f : 32 * f + 32], 0.0), axis=0, keepdims=True)
            held[f, pl.ds(2 * pair, 1), :] = value[:, 0:128]
            held[f, pl.ds(2 * pair + 1, 1), :] = value[:, 128:256]
        return carry

    lax.fori_loop(0, 32, step, 0)
    for f in range(feats):
        out_ref[pl.ds(f, 64, stride=feats), :] = held[f]


def place_kernel(table_ref, view_ref, index_ref, grad_ref, out_ref, total):
    total[...] = jnp.zeros_like(total)
    rows = feats * 32

    def step(pair, carry):
        index = jnp.concatenate(
            [index_ref[pl.ds(2 * pair, 1), :], index_ref[pl.ds(2 * pair + 1, 1), :]], axis=1
        )
        level = (index >> 7) & 31
        keep = iota((32, 256), 0) == level
        parts = [[], []]
        for f in range(feats):
            value = jnp.concatenate(
                [
                    grad_ref[pl.ds(2 * pair * feats + f, 1), :],
                    grad_ref[pl.ds((2 * pair + 1) * feats + f, 1), :],
                ],
                axis=1,
            )
            for part, piece in enumerate(pieces(value, 2)):
                parts[part].append(jnp.where(keep, piece, 0.0).astype(bf16))
        hot = slot_hot(index)
        for part in parts:
            total[...] += lax.dot_general(
                jnp.concatenate(part, axis=0),
                hot,
                (((1,), (1,)), ((), ())),
                preferred_element_type=f32,
            )
        return carry

    lax.fori_loop(0, 32, step, 0)
    lane = iota((8, 128), 1)
    camera = jnp.zeros((8, 128), f32)
    for i in range(8):
        camera = jnp.where(lane == i, table_ref[view_ref[0], i], camera)
    for half in range(2):
        row = half * half_rows
        out_ref[row : row + rows, :] = total[:, 128 * half : 128 * half + 128]
        out_ref[row + rows : row + rows + 8, :] = camera


def render_kernel(
    plan_ref, length_ref, rows_ref, cot_ref, image_ref, out_ref, coef, turned, alphas, weights, moments, shades
):
    lane_tile = iota((8, 128), 1) & 15
    lane_step = iota((8, 128), 1) >> 4
    center_u = jnp.zeros((8, 128), f32)
    center_v = jnp.zeros((8, 128), f32)
    length = jnp.zeros((8, 128), jnp.int32)
    for t in range(16):
        tile = plan_ref[0, t]
        down = tile // 120
        across = tile - down * 120
        at_u = (across * 16 + 8 - 960).astype(f32)
        at_v = (down * 16 + 8 - 540).astype(f32)
        center_u = jnp.where(lane_tile == t, at_u, center_u)
        center_v = jnp.where(lane_tile == t, at_v, center_v)
        length = jnp.where(lane_tile == t, length_ref[0, t], length)
    center_u = center_u / 540.0
    center_v = center_v / 540.0

    def feature(i, f):
        return rows_ref[pl.ds(i * (8 * feats) + f, 8, stride=feats), :]

    coef[...] = jnp.zeros_like(coef)

    def prepare(i, carry):
        off_u = (feature(i, 0) - center_u) * unit
        off_v = (feature(i, 1) - center_v) * unit
        quad_u = feature(i, 2) * (-0.5 * log2e / (unit * unit))
        quad_m = feature(i, 3) * (-log2e / (unit * unit))
        quad_v = feature(i, 4) * (-0.5 * log2e / (unit * unit))
        lead = quad_u * off_u + quad_m * off_v
        base = off_u * lead + quad_v * off_v * off_v + feature(i, 5) * log2e
        alive = (iota((8, 128), 0) + 8 * i) * 8 + lane_step < length
        values = [
            jnp.where(alive, base, -30000.0),
            jnp.where(alive, -(lead + quad_u * off_u), 0.0),
            jnp.where(alive, -(2.0 * quad_v * off_v + quad_m * off_u), 0.0),
            jnp.where(alive, quad_u, 0.0),
            jnp.where(alive, quad_m, 0.0),
            jnp.where(alive, quad_v, 0.0),
            feature(i, 6),
            feature(i, 7),
            feature(i, 8),
        ]
        for m, value in enumerate(values):
            coef[pl.ds(i * 128 + m, 8, stride=16), :] = value
        return carry

    lax.fori_loop(0, 8, prepare, 0)

    def monomials(shape):
        row = iota(shape, 0) & 15
        pixel = iota(shape, 1)
        at_x = ((pixel & 15) * 2 - 15).astype(f32)
        at_y = ((pixel >> 4) * 2 - 15).astype(f32)
        out = jnp.where(row == 0, 1.0, 0.0)
        out = jnp.where(row == 1, at_x, out)
        out = jnp.where(row == 2, at_y, out)
        out = jnp.where(row == 3, at_x * at_x, out)
        out = jnp.where(row == 4, at_x * at_y, out)
        return jnp.where(row == 5, at_y * at_y, out)

    terms = jnp.where(iota((64, 256), 0) >= 16, monomials((64, 256)), 0.0).astype(bf16)
    moment_terms = monomials((16, 256)).astype(bf16)
    cots = [cot_ref[h] for h in range(3)]
    cot_parts = [pieces(cot, 2) for cot in cots]
    cot_high = jnp.concatenate([p[0] for p in cot_parts], axis=0).astype(bf16)
    cot_low = jnp.concatenate([p[1] for p in cot_parts], axis=0).astype(bf16)
    cot_both = jnp.concatenate([cot_high, cot_low], axis=0)
    same_tile = (iota((48, 256), 0) & 15) == (iota((48, 256), 1) & 15)
    across = (((1,), (1,)), ((), ()))

    def forward(i, clear):
        blocks = []
        for own in range(2):
            raw = coef[pl.ds(pl.multiple_of(i * 32 + own * 16, 16), 16), :]
            blocks.append(jnp.concatenate([raw] + pieces(raw, 3), axis=0).T)
        block = jnp.concatenate(blocks, axis=0)
        base = pl.multiple_of(i * 256, 256)
        turned[pl.ds(base, 256), :] = block
        power = jnp.dot(block.astype(bf16), terms, preferred_element_type=f32)
        alpha = jnp.exp2(power)
        alphas[pl.ds(base, 256), :] = alpha
        pieces_w = []
        for k in range(16):
            weight = alpha[16 * k : 16 * k + 16] * clear
            clear = clear - weight
            pieces_w.append(weight)
        weight = jnp.concatenate(pieces_w, axis=0)
        weights[pl.ds(base, 256), :] = weight
        top = weight.astype(bf16)
        low = (weight - top.astype(f32)).astype(bf16)
        both = lax.dot_general(cot_both, top, across, preferred_element_type=f32)
        shade = both[0:48] + both[48:96]
        shade += lax.dot_general(cot_high, low, across, preferred_element_type=f32)
        shade = jnp.where(same_tile, shade, 0.0)
        for h in range(3):
            value = jnp.sum(shade[16 * h : 16 * h + 16], axis=0, keepdims=True)
            for own in range(2):
                shades[h, pl.ds(2 * i + own, 1), :] = value[:, 128 * own : 128 * own + 128]
        return clear

    lax.fori_loop(0, 32, forward, jnp.ones((16, 256), f32))

    def backward(step, behind):
        i = 31 - step
        base = pl.multiple_of(i * 256, 256)
        behind = list(behind)
        pieces_d = [None] * 16
        for k in range(15, -1, -1):
            rows = pl.ds(base + 16 * k, 16)
            alpha = alphas[rows, :]
            pull = None
            for h in range(3):
                gap = turned[rows, 6 + h : 7 + h] - behind[h]
                behind[h] = behind[h] + alpha * gap
                pull = cots[h] * gap if pull is None else pull + cots[h] * gap
            pieces_d[k] = weights[rows, :] * pull
        slope = jnp.concatenate(pieces_d, axis=0)
        top = slope.astype(bf16)
        low = (slope - top.astype(f32)).astype(bf16)
        moment = lax.dot_general(moment_terms, top, across, preferred_element_type=f32)
        moment += lax.dot_general(moment_terms, low, across, preferred_element_type=f32)
        for own in range(2):
            moments[pl.ds(pl.multiple_of(i * 32 + own * 16, 16), 16), :] = moment[
                :, 128 * own : 128 * own + 128
            ]
        return tuple(behind)

    blank = jnp.zeros((16, 256), f32)
    image = lax.fori_loop(0, 32, backward, (blank, blank, blank))
    for h in range(3):
        image_ref[h] = image[h]

    def finish(i, carry):
        off_u = (feature(i, 0) - center_u) * unit
        off_v = (feature(i, 1) - center_v) * unit
        m_one, m_x, m_y, m_xx, m_xy, m_yy = [
            moments[pl.ds(i * 128 + m, 8, stride=16), :] for m in range(6)
        ]
        n_x = m_x - off_u * m_one
        n_y = m_y - off_v * m_one
        n_xx = m_xx - off_u * (m_x + n_x)
        n_xy = m_xy - off_u * m_y - off_v * n_x
        n_yy = m_yy - off_v * (m_y + n_y)
        values = [
            (feature(i, 2) * n_x + feature(i, 3) * n_y) * (1.0 / unit),
            (feature(i, 3) * n_x + feature(i, 4) * n_y) * (1.0 / unit),
            n_xx * (-0.5 / (unit * unit)),
            n_xy * (-1.0 / (unit * unit)),
            n_yy * (-0.5 / (unit * unit)),
            m_one,
        ]
        for h in range(3):
            values.append(shades[h, pl.ds(pl.multiple_of(i * 8, 8), 8), :])
        for f, value in enumerate(values):
            out_ref[pl.ds(i * (8 * feats) + f, 8, stride=feats), :] = value
        return carry

    lax.fori_loop(0, 8, finish, 0)


def gradient_kernel(gauss_ref, own_ref, left_ref, right_ref, far_low_ref, far_high_ref, out_ref, spread, held):
    spread_rows(gauss_ref, spread)
    for half in range(2):
        far_ref = (far_low_ref, far_high_ref)[half]
        sources = [
            (own_ref, half * half_rows),
            (left_ref, half * half_rows),
            (right_ref, half * half_rows),
            (far_ref, 0),
        ]
        views = []
        for ref, base in sources:
            line = ref[base + feats * 32 : base + feats * 32 + 8, :]
            views.append(
                view_values([jnp.broadcast_to(line[:, i : i + 1], (8, 128)) for i in range(8)])
            )

        def step(i, carry):
            at = (i + 4 * half) * (8 * pitch)
            params = [spread[pl.ds(at + p, 8, stride=pitch), :] for p in range(params_n)]

            def every(*params):
                shaped = shape_matrix(params)
                out = []
                for view in views:
                    out += project(params, shaped, view)
                return out + [log_opacity(params[10])]

            _, back = jax.vjp(every, *params)
            cots = []
            opaque = None
            for ref, base in sources:
                rows = [ref[pl.ds(base + 32 * f + 8 * i, 8), :] for f in range(feats)]
                cots += rows[:5] + rows[6:]
                opaque = rows[5] if opaque is None else opaque + rows[5]
            grads = back(cots + [opaque])
            for p in range(params_n):
                held[pl.ds(at + p, 8, stride=pitch), :] = grads[p]
            return carry

        lax.fori_loop(0, 4, step, 0)

    def collect(tile, carry):
        column = pl.ds(pl.multiple_of(tile * 128, 128), 128)
        row = pl.multiple_of(tile * pitch, 8)
        out_ref[0:56, column] = held[pl.ds(row, 56), :]
        out_ref[56:59, column] = held[pl.ds(row + 56, 3), :]
        return carry

    lax.fori_loop(0, 64, collect, 0, unroll=4)


def call(kernel, out, args, specs, scratch, limit=48):
    return pl.pallas_call(
        kernel,
        out_shape=out,
        in_specs=specs,
        out_specs=jax.tree.map(lambda _: vmem, out),
        scratch_shapes=scratch,
        compiler_params=pltpu.CompilerParams(vmem_limit_bytes=limit * 1024 * 1024),
    )(*args)


def exchange(rows, width):
    parts = rows.reshape(owners, width, 1, 128)
    parts = lax.all_to_all(parts, "space", split_axis=0, concat_axis=0, tiled=True)
    return parts.reshape(owners * width, 128)


def per_device(
    gaussians, camera_table, view_camera, tile_plan, requests, tile_lists, tile_lengths, pixel_grad
):
    shape = jax.ShapeDtypeStruct
    ordered = call(
        order_kernel,
        shape((64, 128), jnp.int32),
        (requests[0, 0], tile_lists[0]),
        [vmem, vmem],
        [pltpu.VMEM((512, 128), f32)],
    )
    incoming = exchange(ordered, 1)
    spread = pltpu.VMEM((64 * pitch, 128), f32)
    table = call(
        project_kernel,
        shape((3 * feats * 32, 256), bf16),
        (camera_table, view_camera, gaussians),
        [smem, smem, vmem],
        [spread, pltpu.VMEM((feats, 64, 128), f32)],
    )
    picked = call(
        pick_kernel,
        shape((64 * feats, 128), f32),
        (incoming, table),
        [vmem, vmem],
        [pltpu.VMEM((feats, 64, 128), f32)],
    )
    arrived = exchange(picked, feats)
    image, row_grad = call(
        render_kernel,
        (shape((3, 16, 256), f32), shape((64 * feats, 128), f32)),
        (tile_plan, tile_lengths, arrived, jnp.transpose(pixel_grad[0], (1, 0, 2))),
        [smem, smem, vmem, vmem],
        [
            pltpu.VMEM((1024, 128), f32),
            pltpu.VMEM((8192, 64), f32),
            pltpu.VMEM((8192, 256), f32),
            pltpu.VMEM((8192, 256), f32),
            pltpu.VMEM((1024, 128), f32),
            pltpu.VMEM((3, 64, 128), f32),
        ],
    )
    returned = exchange(row_grad, feats)
    own = call(
        place_kernel,
        shape((2 * half_rows, 128), f32),
        (camera_table, view_camera, incoming, returned),
        [smem, smem, vmem, vmem],
        [pltpu.VMEM((feats * 32, 256), f32)],
    )
    ahead = [(i, (i + 1) % 4) for i in range(4)]
    behind = [(i, (i - 1) % 4) for i in range(4)]
    left = lax.ppermute(own, "view", ahead)
    right = lax.ppermute(own, "view", behind)
    far_low = lax.ppermute(left[:half_rows], "view", ahead)
    far_high = lax.ppermute(right[half_rows:], "view", behind)
    total = call(
        gradient_kernel,
        shape((params_n, slots), f32),
        (gaussians, own, left, right, far_low, far_high),
        [vmem] * 6,
        [spread, spread],
    )
    return (jnp.transpose(image, (1, 0, 2))[None], total)


def solution(mesh):
    placed = (
        P(None, "space"),
        P(),
        P("view"),
        P("view", "space"),
        P("view", "space", None, None),
        P("view", "space", None),
        P("view", "space"),
        P("view", "space", None, None),
    )
    return jax.shard_map(
        per_device,
        mesh=mesh,
        in_specs=placed,
        out_specs=(P("view", "space", None, None), P(None, "space")),
        check_vma=False,
    )
```

```python
import jax
import jax.numpy as jnp
from jax import lax
from jax.experimental import pallas as pl
from jax.experimental.pallas import tpu as pltpu
from jax.sharding import PartitionSpec as P

sh_zero = 0.28209479177387814
sh_one = 0.4886025119029199
sh_two = (
    1.0925484305920792,
    -1.0925484305920792,
    0.31539156525252005,
    -1.0925484305920792,
    0.5462742152960396,
)
sh_three = (
    -0.5900435899266435,
    2.890611442640554,
    -0.4570457994644658,
    0.3731763325901154,
    -0.4570457994644658,
    1.445305721320277,
    -0.5900435899266435,
)
dilation = 0.3 / 291600.0
log2e = 1.4426950408889634
unit = 1080.0
params_n = 59
feats = 9
owners = 64
slots = 8192
pitch = 72
half_rows = 296
lay_unroll = 4
forward_unroll = 8
backward_unroll = 8
pick_unroll = 8
vmem = pl.BlockSpec(memory_space=pltpu.VMEM)
smem = pl.BlockSpec(memory_space=pltpu.SMEM)
f32 = jnp.float32
bf16 = jnp.bfloat16


def quat_matrix(quat_w, quat_x, quat_y, quat_z):
    inv = 1.0 / jnp.sqrt(
        quat_w * quat_w + quat_x * quat_x + quat_y * quat_y + quat_z * quat_z
    )
    unit_w = quat_w * inv
    unit_x = quat_x * inv
    unit_y = quat_y * inv
    unit_z = quat_z * inv
    return [
        [
            1.0 - 2.0 * (unit_y * unit_y + unit_z * unit_z),
            2.0 * (unit_x * unit_y - unit_w * unit_z),
            2.0 * (unit_x * unit_z + unit_w * unit_y),
        ],
        [
            2.0 * (unit_x * unit_y + unit_w * unit_z),
            1.0 - 2.0 * (unit_x * unit_x + unit_z * unit_z),
            2.0 * (unit_y * unit_z - unit_w * unit_x),
        ],
        [
            2.0 * (unit_x * unit_z - unit_w * unit_y),
            2.0 * (unit_y * unit_z + unit_w * unit_x),
            1.0 - 2.0 * (unit_x * unit_x + unit_y * unit_y),
        ],
    ]


def sh_basis(dir_x, dir_y, dir_z):
    sq_x = dir_x * dir_x
    sq_y = dir_y * dir_y
    sq_z = dir_z * dir_z
    return [
        sh_zero,
        -sh_one * dir_y,
        sh_one * dir_z,
        -sh_one * dir_x,
        sh_two[0] * dir_x * dir_y,
        sh_two[1] * dir_y * dir_z,
        sh_two[2] * (2.0 * sq_z - sq_x - sq_y),
        sh_two[3] * dir_x * dir_z,
        sh_two[4] * (sq_x - sq_y),
        sh_three[0] * dir_y * (3.0 * sq_x - sq_y),
        sh_three[1] * dir_x * dir_y * dir_z,
        sh_three[2] * dir_y * (4.0 * sq_z - sq_x - sq_y),
        sh_three[3] * dir_z * (2.0 * sq_z - 3.0 * sq_x - 3.0 * sq_y),
        sh_three[4] * dir_x * (4.0 * sq_z - sq_x - sq_y),
        sh_three[5] * dir_z * (sq_x - sq_y),
        sh_three[6] * dir_x * (sq_x - 3.0 * sq_y),
    ]


def shape_matrix(params):
    scales = [jnp.exp(params[0]), jnp.exp(params[1]), jnp.exp(params[2])]
    own_rot = quat_matrix(params[3], params[4], params[5], params[6])
    return [[own_rot[i][k] * scales[k] for k in range(3)] for i in range(3)]


def view_values(camera):
    view_rot = quat_matrix(camera[0], camera[1], camera[2], camera[3])
    offset_cam = [camera[4], camera[5], camera[6]]
    back = [sum(view_rot[j][i] * offset_cam[j] for j in range(3)) for i in range(3)]
    return view_rot, offset_cam, camera[7], back


def project(center, shaped, harmonics, view):
    view_rot, offset_cam, focal_len, back = view
    in_camera = [
        sum(view_rot[i][j] * center[j] for j in range(3)) + offset_cam[i] for i in range(3)
    ]
    turned = [
        [sum(view_rot[i][j] * shaped[j][k] for j in range(3)) for k in range(3)] for i in range(3)
    ]
    inv_depth = 1.0 / in_camera[2]
    near = focal_len * inv_depth
    screen_u = near * in_camera[0]
    screen_v = near * in_camera[1]
    slope_u = screen_u * inv_depth
    slope_v = screen_v * inv_depth
    jac_u = [near * turned[0][k] - slope_u * turned[2][k] for k in range(3)]
    jac_v = [near * turned[1][k] - slope_v * turned[2][k] for k in range(3)]
    cov_uu = sum(jac_u[k] * jac_u[k] for k in range(3)) + dilation
    cov_uv = sum(jac_u[k] * jac_v[k] for k in range(3))
    cov_vv = sum(jac_v[k] * jac_v[k] for k in range(3)) + dilation
    inv_det = 1.0 / (cov_uu * cov_vv - cov_uv * cov_uv)
    toward = [center[i] + back[i] for i in range(3)]
    inv_len = 1.0 / jnp.sqrt(
        toward[0] * toward[0] + toward[1] * toward[1] + toward[2] * toward[2]
    )
    basis = sh_basis(toward[0] * inv_len, toward[1] * inv_len, toward[2] * inv_len)
    colors = [0.5 + sum(basis[k] * harmonics[3 * k + h] for k in range(16)) for h in range(3)]
    return [
        screen_u,
        screen_v,
        cov_vv * inv_det,
        -cov_uv * inv_det,
        cov_uu * inv_det,
    ] + colors


def log_opacity(logit):
    return jnp.minimum(logit, 0.0) - jnp.log1p(jnp.exp(-jnp.abs(logit)))


def pieces(value, count):
    out = []
    for _ in range(count - 1):
        top = value.astype(bf16).astype(f32)
        out.append(top)
        value = value - top
    out.append(value.astype(bf16).astype(f32))
    return out


def iota(shape, axis):
    return lax.broadcasted_iota(jnp.int32, shape, axis)


def spread_rows(gauss_ref, spread):
    def step(tile, carry):
        column = pl.ds(pl.multiple_of(tile * 128, 128), 128)
        row = pl.multiple_of(tile * pitch, 8)
        spread[pl.ds(row, 56), :] = gauss_ref[0:56, column]
        spread[pl.ds(row + 56, 3), :] = gauss_ref[56:59, column]
        return carry

    lax.fori_loop(0, 64, step, 0, unroll=4)


def order_kernel(requests_ref, lists_ref, out_ref, turned):
    lists = lists_ref[...].astype(f32)
    turned[...] = jnp.concatenate([lists, jnp.zeros((112, 512), f32)], axis=0).T
    group = iota((64, 128), 1) // 16
    entry = jnp.zeros((64, 128), f32)
    for j in range(8):
        piece = turned[pl.ds(j, 64, stride=8), :]
        if j:
            piece = pltpu.roll(piece, 16 * j, 1)
        entry = jnp.where(group == j, piece, entry)
    place = entry.astype(jnp.int32) & 127
    out_ref[...] = jnp.take_along_axis(requests_ref[...], place, axis=1)


def camera_values(table_ref, view_ref):
    row = view_ref[0]
    return [jnp.full((8, 128), table_ref[row, i], f32) for i in range(8)]


def project_kernel(table_ref, view_ref, gauss_ref, out_ref, spread, held):
    view = view_values(camera_values(table_ref, view_ref))
    spread_rows(gauss_ref, spread)

    def step(i, carry):
        at = i * (8 * pitch)
        params = [spread[pl.ds(at + p, 8, stride=pitch), :] for p in range(params_n)]
        shaped = shape_matrix(params[3:10])
        for k in range(9):
            spread[pl.ds(at + params_n + k, 8, stride=pitch), :] = shaped[k // 3][k % 3]
        out = project(params[0:3], shaped, params[11:], view)
        out = out[:5] + [log_opacity(params[10])] + out[5:]
        for f in range(feats):
            held[f, pl.ds(pl.multiple_of(i * 8, 8), 8), :] = out[f]
        return carry

    lax.fori_loop(0, 8, step, 0)
    for f in range(feats):
        for part, value in enumerate(pieces(held[f], 3 if f < 2 else 2)):
            row = (part * feats + f) * 32
            out_ref[row : row + 32, 0:128] = value[0:32].astype(bf16)
            out_ref[row : row + 32, 128:256] = value[32:64].astype(bf16)


def slot_hot(index):
    place = (index >> 12) * 128 + (index & 127)
    return (iota((256, index.shape[1]), 0) == place).astype(f32).astype(bf16)


def pick_rows(index_ref, table_ref, held, third):
    rows = feats * 32

    def step(pair, carry):
        index = jnp.concatenate(
            [index_ref[pl.ds(2 * pair, 1), :], index_ref[pl.ds(2 * pair + 1, 1), :]], axis=1
        )
        got = jnp.dot(table_ref[...], slot_hot(index), preferred_element_type=f32)
        level = (index >> 7) & 31
        keep = iota((32, 256), 0) == level
        for f in range(feats):
            value = got[32 * f : 32 * f + 32] + got[rows + 32 * f : rows + 32 * f + 32]
            if f < third:
                value += got[2 * rows + 32 * f : 2 * rows + 32 * f + 32]
            value = jnp.sum(jnp.where(keep, value, 0.0), axis=0, keepdims=True)
            held(f, 2 * pair, value[:, 0:128])
            held(f, 2 * pair + 1, value[:, 128:256])
        return carry

    lax.fori_loop(0, index_ref.shape[0] // 2, step, 0, unroll=pick_unroll)


def pick_kernel(index_ref, table_ref, out_ref, held):
    def keep(f, row, value):
        held[f, pl.ds(row, 1), :] = value

    pick_rows(index_ref, table_ref, keep, 2)
    for f in range(feats):
        out_ref[pl.ds(f, 64, stride=feats), :] = held[f]


def inverse_kernel(index_ref, out_ref, total):
    total[...] = jnp.zeros_like(total)

    def step(pair, carry):
        index = jnp.concatenate(
            [index_ref[pl.ds(2 * pair, 1), :], index_ref[pl.ds(2 * pair + 1, 1), :]], axis=1
        )
        keep = iota((32, 256), 0) == ((index >> 7) & 31)
        lane = iota((32, 256), 1)
        row = (2 * pair + (lane >> 7)).astype(f32)
        column = (lane & 127).astype(f32)
        both = jnp.concatenate([jnp.where(keep, row, 0.0), jnp.where(keep, column, 0.0)], axis=0)
        total[...] += lax.dot_general(
            both.astype(bf16),
            slot_hot(index),
            (((1,), (1,)), ((), ())),
            preferred_element_type=f32,
        )
        return carry

    lax.fori_loop(0, 32, step, 0, unroll=4)
    spot = (total[0:32] * 128.0 + total[32:64]).astype(jnp.int32)
    out_ref[0:32, :] = spot[:, 0:128]
    out_ref[32:64, :] = spot[:, 128:256]


def place_kernel(camera_ref, view_ref, index_ref, grad_ref, low_ref, high_ref, table):
    for f in range(feats):
        value = grad_ref[pl.ds(f, 64, stride=feats), :]
        for part, piece in enumerate(pieces(value, 2)):
            row = (part * feats + f) * 32
            table[row : row + 32, 0:128] = piece[0:32].astype(bf16)
            table[row : row + 32, 128:256] = piece[32:64].astype(bf16)
    lane = iota((8, 128), 1)
    camera = jnp.zeros((8, 128), f32)
    for i in range(8):
        camera = jnp.where(lane == i, camera_ref[view_ref[0], i], camera)
    for half, out_ref in enumerate((low_ref, high_ref)):
        out_ref[feats * 32 :, :] = camera

        def keep(f, row, value, out_ref=out_ref):
            out_ref[pl.ds(f * 32 + row, 1), :] = value

        pick_rows(index_ref.at[32 * half : 32 * half + 32], table, keep, 0)


def pick(incoming, table):
    return call(
        pick_kernel,
        jax.ShapeDtypeStruct((64 * feats, 128), f32),
        (incoming, table),
        [vmem, vmem],
        [pltpu.VMEM((feats, 64, 128), f32)],
    )


def invert(incoming):
    return call(
        inverse_kernel,
        jax.ShapeDtypeStruct((64, 128), jnp.int32),
        (incoming,),
        [vmem],
        [pltpu.VMEM((64, 256), f32)],
    )


def place(camera_table, view_camera, inverse, returned):
    out = jax.ShapeDtypeStruct((half_rows, 128), f32)
    return call(
        place_kernel,
        (out, out),
        (camera_table, view_camera, inverse, returned),
        [smem, smem, vmem, vmem],
        [pltpu.VMEM((2 * feats * 32, 256), bf16)],
    )


def render_kernel(
    plan_ref, length_ref, rows_ref, cot_ref, image_ref, out_ref, coef, colors, alphas, weights, shades, moments, tints
):
    lane_tile = iota((8, 128), 1) & 15
    lane_step = iota((8, 128), 1) >> 4
    center_u = jnp.zeros((8, 128), f32)
    center_v = jnp.zeros((8, 128), f32)
    length = jnp.zeros((8, 128), jnp.int32)
    for t in range(16):
        tile = plan_ref[0, t]
        down = tile // 120
        across = tile - down * 120
        at_u = (across * 16 + 8 - 960).astype(f32)
        at_v = (down * 16 + 8 - 540).astype(f32)
        center_u = jnp.where(lane_tile == t, at_u, center_u)
        center_v = jnp.where(lane_tile == t, at_v, center_v)
        length = jnp.where(lane_tile == t, length_ref[0, t], length)
    center_u = center_u / 540.0
    center_v = center_v / 540.0

    def feature(i, f):
        return rows_ref[pl.ds(i * (8 * feats) + f, 8, stride=feats), :]

    coef[...] = jnp.zeros_like(coef)

    def prepare(i, carry):
        off_u = (feature(i, 0) - center_u) * unit
        off_v = (feature(i, 1) - center_v) * unit
        quad_u = feature(i, 2) * (-0.5 * log2e / (unit * unit))
        quad_m = feature(i, 3) * (-log2e / (unit * unit))
        quad_v = feature(i, 4) * (-0.5 * log2e / (unit * unit))
        lead = quad_u * off_u + quad_m * off_v
        base = off_u * lead + quad_v * off_v * off_v + feature(i, 5) * log2e
        alive = (iota((8, 128), 0) + 8 * i) * 8 + lane_step < length
        values = [
            jnp.where(alive, base, -30000.0),
            jnp.where(alive, -(lead + quad_u * off_u), 0.0),
            jnp.where(alive, -(2.0 * quad_v * off_v + quad_m * off_u), 0.0),
            jnp.where(alive, quad_u, 0.0),
            jnp.where(alive, quad_m, 0.0),
            jnp.where(alive, quad_v, 0.0),
        ]
        for m, value in enumerate(values):
            coef[pl.ds(i * 64 + m, 8, stride=8), :] = value
        return carry

    lax.fori_loop(0, 8, prepare, 0)

    def monomials(shape):
        row = iota(shape, 0) & 7
        pixel = iota(shape, 1)
        at_x = ((pixel & 15) * 2 - 15).astype(f32)
        at_y = ((pixel >> 4) * 2 - 15).astype(f32)
        out = jnp.where(row == 0, 1.0, 0.0)
        out = jnp.where(row == 1, at_x, out)
        out = jnp.where(row == 2, at_y, out)
        out = jnp.where(row == 3, at_x * at_x, out)
        out = jnp.where(row == 4, at_x * at_y, out)
        return jnp.where(row == 5, at_y * at_y, out)

    terms = jnp.where(iota((32, 256), 0) < 24, monomials((32, 256)), 0.0).astype(bf16)
    moment_terms = monomials((16, 256)).astype(bf16)
    cot_parts = [pieces(cot_ref[h], 2) for h in range(3)]
    cot_high = jnp.concatenate([p[0] for p in cot_parts], axis=0).astype(bf16)
    cot_low = jnp.concatenate([p[1] for p in cot_parts], axis=0).astype(bf16)
    cot_both = jnp.concatenate([cot_high, cot_low], axis=0)
    cot_all = jnp.concatenate([cot_high, cot_high, cot_low], axis=0)
    same_tile = (iota((48, 256), 0) & 15) == (iota((48, 256), 1) & 15)
    own_tile = iota((16, 256), 0) == (iota((16, 256), 1) & 15)
    across = (((1,), (1,)), ((), ()))
    along = (((0,), (0,)), ((), ()))

    def pair(i, ref, row, step):
        return jnp.concatenate(
            [ref[pl.ds(2 * i * step + row, 1), :], ref[pl.ds((2 * i + 1) * step + row, 1), :]],
            axis=1,
        )

    def lay(i, carry):
        raw = jnp.concatenate(
            [
                coef[pl.ds(pl.multiple_of(i * 16, 8), 8), :],
                coef[pl.ds(pl.multiple_of(i * 16 + 8, 8), 8), :],
            ],
            axis=1,
        )
        block = jnp.concatenate(pieces(raw, 3) + [jnp.zeros((8, 256), f32)], axis=0)
        base = pl.multiple_of(i * 256, 256)
        power = lax.dot_general(
            block.astype(bf16), terms, along, preferred_element_type=f32
        )
        alphas[pl.ds(base, 256), :] = jnp.exp2(power)
        high = []
        low = []
        for h in range(3):
            value = jnp.where(own_tile, pair(i, rows_ref, 6 + h, feats), 0.0)
            parts = pieces(value, 2)
            high.append(parts[0])
            low.append(parts[1])
        color = jnp.concatenate(high + low + high, axis=0).astype(bf16)
        colors[i] = color[0:96]
        shades[pl.ds(base, 256), :] = lax.dot_general(
            color, cot_all, along, preferred_element_type=f32
        )
        return carry

    lax.fori_loop(0, 32, lay, 0, unroll=lay_unroll)

    image_ref[...] = jnp.zeros_like(image_ref)

    def forward(i, clear):
        base = pl.multiple_of(i * 256, 256)
        kept = []
        for k in range(16):
            weight = alphas[pl.ds(base + 16 * k, 16), :] * clear
            clear = clear - weight
            kept.append(weight)
        weight = jnp.concatenate(kept, axis=0)
        weights[pl.ds(base, 256), :] = weight
        top = weight.astype(bf16)
        low = (weight - top.astype(f32)).astype(bf16)
        color = colors[i]
        both = jnp.dot(color, top, preferred_element_type=f32)
        image = both[0:48] + both[48:96]
        image += jnp.dot(color[0:48], low, preferred_element_type=f32)
        for h in range(3):
            image_ref[h] += image[16 * h : 16 * h + 16]
        both = lax.dot_general(cot_both, top, across, preferred_element_type=f32)
        tint = both[0:48] + both[48:96]
        tint += lax.dot_general(cot_high, low, across, preferred_element_type=f32)
        tint = jnp.where(same_tile, tint, 0.0)
        for h in range(3):
            value = jnp.sum(tint[16 * h : 16 * h + 16], axis=0, keepdims=True)
            for own in range(2):
                tints[h, pl.ds(2 * i + own, 1), :] = value[:, 128 * own : 128 * own + 128]
        return clear

    lax.fori_loop(0, 32, forward, jnp.ones((16, 256), f32), unroll=forward_unroll)

    def backward(step, behind):
        i = 31 - step
        base = pl.multiple_of(i * 256, 256)
        kept = [None] * 16
        for k in range(15, -1, -1):
            rows = pl.ds(base + 16 * k, 16)
            gap = shades[rows, :] - behind
            kept[k] = weights[rows, :] * gap
            behind = behind + alphas[rows, :] * gap
        slope = jnp.concatenate(kept, axis=0)
        top = slope.astype(bf16)
        low = (slope - top.astype(f32)).astype(bf16)
        moment = lax.dot_general(moment_terms, top, across, preferred_element_type=f32)
        moment += lax.dot_general(moment_terms, low, across, preferred_element_type=f32)
        for own in range(2):
            moments[pl.ds(pl.multiple_of(i * 16 + own * 8, 8), 8), :] = moment[
                0:8, 128 * own : 128 * own + 128
            ]
        return behind

    lax.fori_loop(0, 32, backward, jnp.zeros((16, 256), f32), unroll=backward_unroll)

    def finish(i, carry):
        off_u = (feature(i, 0) - center_u) * unit
        off_v = (feature(i, 1) - center_v) * unit
        m_one, m_x, m_y, m_xx, m_xy, m_yy = [
            moments[pl.ds(i * 64 + m, 8, stride=8), :] for m in range(6)
        ]
        n_x = m_x - off_u * m_one
        n_y = m_y - off_v * m_one
        n_xx = m_xx - off_u * (m_x + n_x)
        n_xy = m_xy - off_u * m_y - off_v * n_x
        n_yy = m_yy - off_v * (m_y + n_y)
        values = [
            (feature(i, 2) * n_x + feature(i, 3) * n_y) * (1.0 / unit),
            (feature(i, 3) * n_x + feature(i, 4) * n_y) * (1.0 / unit),
            n_xx * (-0.5 / (unit * unit)),
            n_xy * (-1.0 / (unit * unit)),
            n_yy * (-0.5 / (unit * unit)),
            m_one,
        ]
        for h in range(3):
            values.append(tints[h, pl.ds(pl.multiple_of(i * 8, 8), 8), :])
        for f, value in enumerate(values):
            out_ref[pl.ds(i * (8 * feats) + f, 8, stride=feats), :] = value
        return carry

    lax.fori_loop(0, 8, finish, 0)


def render(tile_plan, tile_lengths, arrived, cots):
    shape = jax.ShapeDtypeStruct
    return call(
        render_kernel,
        (shape((3, 16, 256), f32), shape((64 * feats, 128), f32)),
        (tile_plan, tile_lengths, arrived, cots),
        [smem, smem, vmem, vmem],
        [
            pltpu.VMEM((512, 128), f32),
            pltpu.VMEM((32, 96, 256), bf16),
            pltpu.VMEM((8192, 256), f32),
            pltpu.VMEM((8192, 256), f32),
            pltpu.VMEM((8192, 256), f32),
            pltpu.VMEM((512, 128), f32),
            pltpu.VMEM((3, 64, 128), f32),
        ],
    )


def source_views(refs):
    sources = []
    for low, high in zip(refs[0::2], refs[1::2]):
        line = low[feats * 32 : feats * 32 + 8, :]
        camera = [jnp.broadcast_to(line[:, i : i + 1], (8, 128)) for i in range(8)]
        sources.append(((low, high), view_values(camera)))
    return sources


def view_gradient(sources, spread, half, step):
    at = (4 * half + step) * (8 * pitch)

    def param(p):
        return spread[pl.ds(at + p, 8, stride=pitch), :]

    center = [param(p) for p in range(3)]
    shaped = [[param(params_n + 3 * j + k) for k in range(3)] for j in range(3)]
    harmonics = [param(p) for p in range(11, params_n)]
    total = None
    for refs, view in sources:
        rows = [refs[half][pl.ds(32 * f + 8 * step, 8), :] for f in range(feats)]

        def one(center, shaped, harmonics, view=view):
            return project(center, shaped, harmonics, view)

        _, back = jax.vjp(one, center, shaped, harmonics)
        d_center, d_shaped, d_harmonics = back(rows[:5] + rows[6:])
        part = d_center + sum(d_shaped, []) + [rows[5]] + d_harmonics
        total = part if total is None else [x + y for x, y in zip(total, part)]
    return total


def first_kernel(spread, low_ref, high_ref, out_ref):
    sources = source_views([low_ref, high_ref])
    for half in range(2):

        def step(i, carry, half=half):
            rows = pl.ds(pl.multiple_of(32 * half + i * 8, 8), 8)
            for p, value in enumerate(view_gradient(sources, spread, half, i)):
                out_ref[p, rows, :] = value
            return carry

        lax.fori_loop(0, 4, step, 0)


def middle_kernel(spread, left_low, left_high, right_low, right_high, sum_ref, out_ref):
    sources = source_views([left_low, left_high, right_low, right_high])
    for half in range(2):

        def step(i, carry, half=half):
            rows = pl.ds(pl.multiple_of(32 * half + i * 8, 8), 8)
            for p, value in enumerate(view_gradient(sources, spread, half, i)):
                out_ref[p, rows, :] = value + sum_ref[p, rows, :]
            return carry

        lax.fori_loop(0, 4, step, 0)


def last_kernel(spread, low_ref, high_ref, sum_ref, out_ref, held):
    sources = source_views([low_ref, high_ref])
    for half in range(2):

        def step(i, carry, half=half):
            rows = pl.ds(pl.multiple_of(32 * half + i * 8, 8), 8)
            at = (4 * half + i) * (8 * pitch)
            total = view_gradient(sources, spread, half, i)
            total = [value + sum_ref[p, rows, :] for p, value in enumerate(total)]
            params = [spread[pl.ds(at + p, 8, stride=pitch), :] for p in range(3, 11)]
            _, back = jax.vjp(lambda *p: shape_matrix(p), *params[:7])
            d_shape = back([total[3 + 3 * j : 6 + 3 * j] for j in range(3)])
            d_logit = total[12] / (1.0 + jnp.exp(params[7]))
            for p, value in enumerate(total[0:3] + list(d_shape) + [d_logit] + total[13:]):
                held[pl.ds(at + p, 8, stride=pitch), :] = value
            return carry

        lax.fori_loop(0, 4, step, 0)

    def collect(tile, carry):
        column = pl.ds(pl.multiple_of(tile * 128, 128), 128)
        row = pl.multiple_of(tile * pitch, 8)
        out_ref[0:56, column] = held[pl.ds(row, 56), :]
        out_ref[56:59, column] = held[pl.ds(row + 56, 3), :]
        return carry

    lax.fori_loop(0, 64, collect, 0, unroll=4)


def call(kernel, out, args, specs, scratch, limit=48):
    return pl.pallas_call(
        kernel,
        out_shape=out,
        in_specs=specs,
        out_specs=jax.tree.map(lambda _: vmem, out),
        scratch_shapes=scratch,
        compiler_params=pltpu.CompilerParams(vmem_limit_bytes=limit * 1024 * 1024),
    )(*args)


def exchange(rows, width):
    parts = rows.reshape(owners, width, 1, 128)
    parts = lax.all_to_all(parts, "space", split_axis=0, concat_axis=0, tiled=True)
    return parts.reshape(owners * width, 128)


def per_device(
    gaussians, camera_table, view_camera, tile_plan, requests, tile_lists, tile_lengths, pixel_grad
):
    shape = jax.ShapeDtypeStruct
    ordered = call(
        order_kernel,
        shape((64, 128), jnp.int32),
        (requests[0, 0], tile_lists[0]),
        [vmem, vmem],
        [pltpu.VMEM((512, 128), f32)],
    )
    incoming = exchange(ordered, 1)
    table, spread = call(
        project_kernel,
        (shape(((2 * feats + 2) * 32, 256), bf16), shape((64 * pitch, 128), f32)),
        (camera_table, view_camera, gaussians),
        [smem, smem, vmem],
        [pltpu.VMEM((feats, 64, 128), f32)],
    )
    picked = pick(incoming, table)
    arrived = exchange(picked, feats)
    inverse = invert(incoming)
    image, row_grad = render(
        tile_plan, tile_lengths, arrived, jnp.transpose(pixel_grad[0], (1, 0, 2))
    )
    returned = exchange(row_grad, feats)
    low, high = place(camera_table, view_camera, inverse, returned)
    ahead = [(i, (i + 1) % 4) for i in range(4)]
    behind = [(i, (i - 1) % 4) for i in range(4)]
    left_low = lax.ppermute(low, "view", ahead)
    right_high = lax.ppermute(high, "view", behind)
    left_high = lax.ppermute(high, "view", ahead)
    right_low = lax.ppermute(low, "view", behind)
    far_low = lax.ppermute(left_low, "view", ahead)
    far_high = lax.ppermute(right_high, "view", behind)
    part = shape((61, 64, 128), f32)
    total = call(first_kernel, part, (spread, low, high), [vmem] * 3, [])
    total = call(
        middle_kernel,
        part,
        (spread, left_low, left_high, right_low, right_high, total),
        [vmem] * 6,
        [],
    )
    total = call(
        last_kernel,
        shape((params_n, slots), f32),
        (spread, far_low, far_high, total),
        [vmem] * 4,
        [pltpu.VMEM((64 * pitch, 128), f32)],
    )
    return (jnp.transpose(image, (1, 0, 2))[None], total)


def solution(mesh):
    placed = (
        P(None, "space"),
        P(),
        P("view"),
        P("view", "space"),
        P("view", "space", None, None),
        P("view", "space", None),
        P("view", "space"),
        P("view", "space", None, None),
    )
    return jax.shard_map(
        per_device,
        mesh=mesh,
        in_specs=placed,
        out_specs=(P("view", "space", None, None), P(None, "space")),
        check_vma=False,
    )
```

```python
import jax
import jax.numpy as jnp
from jax import lax
from jax.experimental import pallas as pl
from jax.experimental.pallas import tpu as pltpu
from jax.sharding import PartitionSpec as P

sh_zero = 0.28209479177387814
sh_one = 0.4886025119029199
sh_two = (
    1.0925484305920792,
    -1.0925484305920792,
    0.31539156525252005,
    -1.0925484305920792,
    0.5462742152960396,
)
sh_three = (
    -0.5900435899266435,
    2.890611442640554,
    -0.4570457994644658,
    0.3731763325901154,
    -0.4570457994644658,
    1.445305721320277,
    -0.5900435899266435,
)
dilation = 0.3 / 291600.0
log2e = 1.4426950408889634
unit = 1080.0
params_n = 59
feats = 9
owners = 64
slots = 8192
pitch = 72
half_rows = 296
lay_unroll = 16
image_step = 8
colors_at = 8448
forward_unroll = 16
backward_unroll = 16
pick_unroll = 16
vmem = pl.BlockSpec(memory_space=pltpu.VMEM)
smem = pl.BlockSpec(memory_space=pltpu.SMEM)
f32 = jnp.float32
bf16 = jnp.bfloat16


def quat_matrix(quat_w, quat_x, quat_y, quat_z):
    inv = 1.0 / jnp.sqrt(
        quat_w * quat_w + quat_x * quat_x + quat_y * quat_y + quat_z * quat_z
    )
    unit_w = quat_w * inv
    unit_x = quat_x * inv
    unit_y = quat_y * inv
    unit_z = quat_z * inv
    return [
        [
            1.0 - 2.0 * (unit_y * unit_y + unit_z * unit_z),
            2.0 * (unit_x * unit_y - unit_w * unit_z),
            2.0 * (unit_x * unit_z + unit_w * unit_y),
        ],
        [
            2.0 * (unit_x * unit_y + unit_w * unit_z),
            1.0 - 2.0 * (unit_x * unit_x + unit_z * unit_z),
            2.0 * (unit_y * unit_z - unit_w * unit_x),
        ],
        [
            2.0 * (unit_x * unit_z - unit_w * unit_y),
            2.0 * (unit_y * unit_z + unit_w * unit_x),
            1.0 - 2.0 * (unit_x * unit_x + unit_y * unit_y),
        ],
    ]


def sh_basis(dir_x, dir_y, dir_z):
    sq_x = dir_x * dir_x
    sq_y = dir_y * dir_y
    sq_z = dir_z * dir_z
    return [
        sh_zero,
        -sh_one * dir_y,
        sh_one * dir_z,
        -sh_one * dir_x,
        sh_two[0] * dir_x * dir_y,
        sh_two[1] * dir_y * dir_z,
        sh_two[2] * (2.0 * sq_z - sq_x - sq_y),
        sh_two[3] * dir_x * dir_z,
        sh_two[4] * (sq_x - sq_y),
        sh_three[0] * dir_y * (3.0 * sq_x - sq_y),
        sh_three[1] * dir_x * dir_y * dir_z,
        sh_three[2] * dir_y * (4.0 * sq_z - sq_x - sq_y),
        sh_three[3] * dir_z * (2.0 * sq_z - 3.0 * sq_x - 3.0 * sq_y),
        sh_three[4] * dir_x * (4.0 * sq_z - sq_x - sq_y),
        sh_three[5] * dir_z * (sq_x - sq_y),
        sh_three[6] * dir_x * (sq_x - 3.0 * sq_y),
    ]


def shape_matrix(params):
    scales = [jnp.exp(params[0]), jnp.exp(params[1]), jnp.exp(params[2])]
    own_rot = quat_matrix(params[3], params[4], params[5], params[6])
    return [[own_rot[i][k] * scales[k] for k in range(3)] for i in range(3)]


def view_values(camera):
    view_rot = quat_matrix(camera[0], camera[1], camera[2], camera[3])
    offset_cam = [camera[4], camera[5], camera[6]]
    back = [sum(view_rot[j][i] * offset_cam[j] for j in range(3)) for i in range(3)]
    return view_rot, offset_cam, camera[7], back


def project(center, shaped, harmonics, view):
    view_rot, offset_cam, focal_len, back = view
    in_camera = [
        sum(view_rot[i][j] * center[j] for j in range(3)) + offset_cam[i] for i in range(3)
    ]
    turned = [
        [sum(view_rot[i][j] * shaped[j][k] for j in range(3)) for k in range(3)] for i in range(3)
    ]
    inv_depth = 1.0 / in_camera[2]
    near = focal_len * inv_depth
    screen_u = near * in_camera[0]
    screen_v = near * in_camera[1]
    slope_u = screen_u * inv_depth
    slope_v = screen_v * inv_depth
    jac_u = [near * turned[0][k] - slope_u * turned[2][k] for k in range(3)]
    jac_v = [near * turned[1][k] - slope_v * turned[2][k] for k in range(3)]
    cov_uu = sum(jac_u[k] * jac_u[k] for k in range(3)) + dilation
    cov_uv = sum(jac_u[k] * jac_v[k] for k in range(3))
    cov_vv = sum(jac_v[k] * jac_v[k] for k in range(3)) + dilation
    inv_det = 1.0 / (cov_uu * cov_vv - cov_uv * cov_uv)
    toward = [center[i] + back[i] for i in range(3)]
    inv_len = 1.0 / jnp.sqrt(
        toward[0] * toward[0] + toward[1] * toward[1] + toward[2] * toward[2]
    )
    basis = sh_basis(toward[0] * inv_len, toward[1] * inv_len, toward[2] * inv_len)
    colors = [0.5 + sum(basis[k] * harmonics[3 * k + h] for k in range(16)) for h in range(3)]
    return [
        screen_u,
        screen_v,
        cov_vv * inv_det,
        -cov_uv * inv_det,
        cov_uu * inv_det,
    ] + colors


def log_opacity(logit):
    return jnp.minimum(logit, 0.0) - jnp.log1p(jnp.exp(-jnp.abs(logit)))


def pieces(value, count):
    out = []
    for _ in range(count - 1):
        top = value.astype(bf16).astype(f32)
        out.append(top)
        value = value - top
    out.append(value.astype(bf16).astype(f32))
    return out


def iota(shape, axis):
    return lax.broadcasted_iota(jnp.int32, shape, axis)


def order_kernel(requests_hbm, lists_hbm, out_ref, requests, lists, turned, sems):
    copies = [
        pltpu.make_async_copy(lists_hbm, lists.at[0:16], sems.at[0]),
        pltpu.make_async_copy(requests_hbm, requests, sems.at[1]),
    ]
    for copy in copies:
        copy.start()
    lists[16:128] = jnp.zeros((112, 512), jnp.int32)
    for copy in copies:
        copy.wait()
    turned[...] = lists[...].T
    group = iota((64, 128), 1) // 16
    entry = jnp.zeros((64, 128), jnp.int32)
    for j in range(8):
        piece = turned[pl.ds(j, 64, stride=8), :]
        if j:
            piece = pltpu.roll(piece, 16 * j, 1)
        entry = jnp.where(group == j, piece, entry)
    out_ref[...] = jnp.take_along_axis(requests[...], entry & 127, axis=1)


def camera_values(table_ref, view_ref):
    row = view_ref[0]
    return [jnp.full((8, 128), table_ref[i, row], f32) for i in range(8)]


def tile_frame(plan_ref, length_ref):
    lane_tile = iota((8, 128), 1) & 15
    center_u = jnp.zeros((8, 128), f32)
    center_v = jnp.zeros((8, 128), f32)
    length = jnp.zeros((8, 128), jnp.int32)
    for t in range(16):
        tile = plan_ref[0, t]
        down = tile // 120
        across = tile - down * 120
        at_u = (across * 16 + 8 - 960).astype(f32)
        at_v = (down * 16 + 8 - 540).astype(f32)
        center_u = jnp.where(lane_tile == t, at_u, center_u)
        center_v = jnp.where(lane_tile == t, at_v, center_v)
        length = jnp.where(lane_tile == t, length_ref[0, t], length)
    return center_u / 540.0, center_v / 540.0, length


def project_kernel(
    table_ref, view_ref, gauss_hbm, out_ref, spread, gauss, held, sems
):
    def fetch(i):
        column = pl.ds(pl.multiple_of(i * 1024, 1024), 1024)
        return pltpu.make_async_copy(gauss_hbm.at[:, column], gauss.at[:, column], sems.at[i])

    for i in range(8):
        fetch(i).start()
    view = view_values(camera_values(table_ref, view_ref))

    def step(i, carry):
        at = i * (8 * pitch)
        fetch(i).wait()
        for tile in range(8):
            column = pl.ds(pl.multiple_of(i * 1024 + tile * 128, 128), 128)
            row = pl.multiple_of(at + tile * pitch, 8)
            spread[pl.ds(row, 56), :] = gauss[0:56, column]
            spread[pl.ds(row + 56, 3), :] = gauss[56:59, column]
        params = [spread[pl.ds(at + p, 8, stride=pitch), :] for p in range(params_n)]
        shaped = shape_matrix(params[3:10])
        for k in range(9):
            spread[pl.ds(at + params_n + k, 8, stride=pitch), :] = shaped[k // 3][k % 3]
        out = project(params[0:3], shaped, params[11:], view)
        out = out[:5] + [log_opacity(params[10])] + out[5:]
        for f in range(feats):
            held[f, pl.ds(pl.multiple_of(i * 8, 8), 8), :] = out[f]
        return carry

    lax.fori_loop(0, 8, step, 0)
    for f in range(feats):
        for part, value in enumerate(pieces(held[f], 3 if f < 2 else 2)):
            row = (part * feats + f) * 32
            out_ref[row : row + 32, 0:128] = value[0:32].astype(bf16)
            out_ref[row : row + 32, 128:256] = value[32:64].astype(bf16)


def slot_hot(index):
    place = (index >> 12) * 128 + (index & 127)
    return (iota((256, index.shape[1]), 0) == place).astype(f32).astype(bf16)


def pick_rows(index_ref, table_ref, held, third):
    rows = feats * 32

    def step(pair, carry):
        index = jnp.concatenate(
            [index_ref[pl.ds(2 * pair, 1), :], index_ref[pl.ds(2 * pair + 1, 1), :]], axis=1
        )
        got = jnp.dot(table_ref[...], slot_hot(index), preferred_element_type=f32)
        level = (index >> 7) & 31
        keep = iota((32, 256), 0) == level
        for f in range(feats):
            value = got[32 * f : 32 * f + 32] + got[rows + 32 * f : rows + 32 * f + 32]
            if f < third:
                value += got[2 * rows + 32 * f : 2 * rows + 32 * f + 32]
            value = jnp.sum(jnp.where(keep, value, 0.0), axis=0, keepdims=True)
            held(f, 2 * pair, value[:, 0:128])
            held(f, 2 * pair + 1, value[:, 128:256])
        return carry

    lax.fori_loop(0, index_ref.shape[0] // 2, step, 0, unroll=pick_unroll)


def pick_kernel(index_ref, table_ref, out_ref, held):
    def keep(f, row, value):
        held[f, pl.ds(row, 1), :] = value

    pick_rows(index_ref, table_ref, keep, 2)
    for f in range(feats):
        out_ref[pl.ds(f, 64, stride=feats), :] = held[f]


def inverse_kernel(index_ref, out_ref, total):
    total[...] = jnp.zeros_like(total)

    def step(pair, carry):
        index = jnp.concatenate(
            [index_ref[pl.ds(2 * pair, 1), :], index_ref[pl.ds(2 * pair + 1, 1), :]], axis=1
        )
        keep = iota((32, 256), 0) == ((index >> 7) & 31)
        lane = iota((32, 256), 1)
        row = (2 * pair + (lane >> 7)).astype(f32)
        column = (lane & 127).astype(f32)
        both = jnp.concatenate([jnp.where(keep, row, 0.0), jnp.where(keep, column, 0.0)], axis=0)
        total[...] += lax.dot_general(
            both.astype(bf16),
            slot_hot(index),
            (((1,), (1,)), ((), ())),
            preferred_element_type=f32,
        )
        return carry

    lax.fori_loop(0, 32, step, 0, unroll=4)
    spot = (total[0:32] * 128.0 + total[32:64]).astype(jnp.int32)
    out_ref[0:32, :] = spot[:, 0:128]
    out_ref[32:64, :] = spot[:, 128:256]


def place_kernel(camera_ref, view_ref, index_ref, grad_ref, low_ref, high_ref, table):
    for f in range(feats):
        value = grad_ref[pl.ds(f, 64, stride=feats), :]
        for part, piece in enumerate(pieces(value, 2)):
            row = (part * feats + f) * 32
            table[row : row + 32, 0:128] = piece[0:32].astype(bf16)
            table[row : row + 32, 128:256] = piece[32:64].astype(bf16)
    lane = iota((8, 128), 1)
    camera = jnp.zeros((8, 128), f32)
    for i in range(8):
        camera = jnp.where(lane == i, camera_ref[i, view_ref[0]], camera)
    for half, out_ref in enumerate((low_ref, high_ref)):
        out_ref[feats * 32 :, :] = camera

        def keep(f, row, value, out_ref=out_ref):
            out_ref[pl.ds(f * 32 + row, 1), :] = value

        pick_rows(index_ref.at[32 * half : 32 * half + 32], table, keep, 0)


def pick(incoming, table):
    return call(
        pick_kernel,
        jax.ShapeDtypeStruct((64 * feats, 128), f32),
        (incoming, table),
        [vmem, vmem],
        [pltpu.VMEM((feats, 64, 128), f32)],
    )


def invert(incoming):
    return call(
        inverse_kernel,
        jax.ShapeDtypeStruct((64, 128), jnp.int32),
        (incoming,),
        [vmem],
        [pltpu.VMEM((64, 256), f32)],
    )


def place(camera_table, view_camera, inverse, returned):
    out = jax.ShapeDtypeStruct((half_rows, 128), f32)
    return call(
        place_kernel,
        (out, out),
        (camera_table, view_camera, inverse, returned),
        [smem, smem, vmem, vmem],
        [pltpu.VMEM((2 * feats * 32, 256), bf16)],
    )


def render_kernel(
    plan_ref,
    length_ref,
    rows_ref,
    cot_ref,
    made_hbm,
    out_ref,
    weights,
    colors,
    coef,
    alphas,
    shades,
    moments,
    tints,
    sems,
):
    lane_step = iota((8, 128), 1) >> 4
    center_u, center_v, length = tile_frame(plan_ref, length_ref)

    def feature(i, f):
        return rows_ref[pl.ds(i * (8 * feats) + f, 8, stride=feats), :]

    coef[...] = jnp.zeros_like(coef)

    def prepare(i, carry):
        off_u = (feature(i, 0) - center_u) * unit
        off_v = (feature(i, 1) - center_v) * unit
        quad_u = feature(i, 2) * (-0.5 * log2e / (unit * unit))
        quad_m = feature(i, 3) * (-log2e / (unit * unit))
        quad_v = feature(i, 4) * (-0.5 * log2e / (unit * unit))
        lead = quad_u * off_u + quad_m * off_v
        base = off_u * lead + quad_v * off_v * off_v + feature(i, 5) * log2e
        alive = (iota((8, 128), 0) + 8 * i) * 8 + lane_step < length
        values = [
            jnp.where(alive, base, -30000.0),
            jnp.where(alive, -(lead + quad_u * off_u), 0.0),
            jnp.where(alive, -(2.0 * quad_v * off_v + quad_m * off_u), 0.0),
            jnp.where(alive, quad_u, 0.0),
            jnp.where(alive, quad_m, 0.0),
            jnp.where(alive, quad_v, 0.0),
        ]
        for m, value in enumerate(values):
            coef[pl.ds(i * 64 + m, 8, stride=8), :] = value
        return carry

    lax.fori_loop(0, 8, prepare, 0)

    def monomials(shape):
        row = iota(shape, 0) & 7
        pixel = iota(shape, 1)
        at_x = ((pixel & 15) * 2 - 15).astype(f32)
        at_y = ((pixel >> 4) * 2 - 15).astype(f32)
        out = jnp.where(row == 0, 1.0, 0.0)
        out = jnp.where(row == 1, at_x, out)
        out = jnp.where(row == 2, at_y, out)
        out = jnp.where(row == 3, at_x * at_x, out)
        out = jnp.where(row == 4, at_x * at_y, out)
        return jnp.where(row == 5, at_y * at_y, out)

    terms = jnp.where(iota((32, 256), 0) < 24, monomials((32, 256)), 0.0).astype(bf16)
    moment_terms = monomials((16, 256)).astype(bf16)
    cot_parts = [pieces(cot_ref[h], 2) for h in range(3)]
    cot_high = jnp.concatenate([p[0] for p in cot_parts], axis=0).astype(bf16)
    cot_low = jnp.concatenate([p[1] for p in cot_parts], axis=0).astype(bf16)
    cot_both = jnp.concatenate([cot_high, cot_low], axis=0)
    cot_all = jnp.concatenate([cot_high, cot_high, cot_low], axis=0)
    same_tile = (iota((48, 256), 0) & 15) == (iota((48, 256), 1) & 15)
    own_tile = iota((16, 256), 0) == (iota((16, 256), 1) & 15)
    across = (((1,), (1,)), ((), ()))
    along = (((0,), (0,)), ((), ()))

    def pair(i, ref, row, step):
        return jnp.concatenate(
            [ref[pl.ds(2 * i * step + row, 1), :], ref[pl.ds((2 * i + 1) * step + row, 1), :]],
            axis=1,
        )

    def lay(i, carry):
        raw = jnp.concatenate(
            [
                coef[pl.ds(pl.multiple_of(i * 16, 8), 8), :],
                coef[pl.ds(pl.multiple_of(i * 16 + 8, 8), 8), :],
            ],
            axis=1,
        )
        block = jnp.concatenate(pieces(raw, 3) + [jnp.zeros((8, 256), f32)], axis=0)
        base = pl.multiple_of(i * 256, 256)
        power = lax.dot_general(
            block.astype(bf16), terms, along, preferred_element_type=f32
        )
        alphas[pl.ds(base, 256), :] = jnp.exp2(power)
        high = []
        low = []
        for h in range(3):
            value = jnp.where(own_tile, pair(i, rows_ref, 6 + h, feats), 0.0)
            parts = pieces(value, 2)
            high.append(parts[0])
            low.append(parts[1])
        color = jnp.concatenate(high + low, axis=0)
        colors[pl.ds(pl.multiple_of(i * 96, 8), 96), :] = color
        color = jnp.concatenate([color] + high, axis=0).astype(bf16)
        shades[pl.ds(base, 256), :] = lax.dot_general(
            color, cot_all, along, preferred_element_type=f32
        )
        return carry

    lax.fori_loop(0, 32, lay, 0, unroll=lay_unroll)

    def store(i):
        rows = pl.ds(pl.multiple_of(i * 256, 256), 256)
        return pltpu.make_async_copy(weights.at[rows], made_hbm.at[rows], sems.at[i])

    store_colors = pltpu.make_async_copy(colors, made_hbm.at[colors_at : colors_at + 3072], sems.at[32])
    store_colors.start()

    def forward(i, clear):
        base = pl.multiple_of(i * 256, 256)
        kept = []
        for k in range(16):
            weight = alphas[pl.ds(base + 16 * k, 16), :] * clear
            clear = clear - weight
            kept.append(weight)
        weight = jnp.concatenate(kept, axis=0)
        weights[pl.ds(base, 256), :] = weight
        store(i).start()
        top = weight.astype(bf16)
        low = (weight - top.astype(f32)).astype(bf16)
        both = lax.dot_general(cot_both, top, across, preferred_element_type=f32)
        tint = both[0:48] + both[48:96]
        tint += lax.dot_general(cot_high, low, across, preferred_element_type=f32)
        tint = jnp.where(same_tile, tint, 0.0)
        for h in range(3):
            value = jnp.sum(tint[16 * h : 16 * h + 16], axis=0, keepdims=True)
            for own in range(2):
                tints[h, pl.ds(2 * i + own, 1), :] = value[:, 128 * own : 128 * own + 128]
        return clear

    lax.fori_loop(0, 32, forward, jnp.ones((16, 256), f32), unroll=forward_unroll)

    def backward(step, behind):
        i = 31 - step
        base = pl.multiple_of(i * 256, 256)
        kept = [None] * 16
        for k in range(15, -1, -1):
            rows = pl.ds(base + 16 * k, 16)
            alpha = alphas[rows, :]
            shown = shades[rows, :]
            kept[k] = weights[rows, :] * (shown - behind)
            behind = (1.0 - alpha) * behind + alpha * shown
        slope = jnp.concatenate(kept, axis=0)
        top = slope.astype(bf16)
        low = (slope - top.astype(f32)).astype(bf16)
        moment = lax.dot_general(moment_terms, top, across, preferred_element_type=f32)
        moment += lax.dot_general(moment_terms, low, across, preferred_element_type=f32)
        for own in range(2):
            moments[pl.ds(pl.multiple_of(i * 16 + own * 8, 8), 8), :] = moment[
                0:8, 128 * own : 128 * own + 128
            ]
        return behind

    lax.fori_loop(0, 32, backward, jnp.zeros((16, 256), f32), unroll=backward_unroll)

    def finish(i, carry):
        off_u = (feature(i, 0) - center_u) * unit
        off_v = (feature(i, 1) - center_v) * unit
        m_one, m_x, m_y, m_xx, m_xy, m_yy = [
            moments[pl.ds(i * 64 + m, 8, stride=8), :] for m in range(6)
        ]
        n_x = m_x - off_u * m_one
        n_y = m_y - off_v * m_one
        n_xx = m_xx - off_u * (m_x + n_x)
        n_xy = m_xy - off_u * m_y - off_v * n_x
        n_yy = m_yy - off_v * (m_y + n_y)
        values = [
            (feature(i, 2) * n_x + feature(i, 3) * n_y) * (1.0 / unit),
            (feature(i, 3) * n_x + feature(i, 4) * n_y) * (1.0 / unit),
            n_xx * (-0.5 / (unit * unit)),
            n_xy * (-1.0 / (unit * unit)),
            n_yy * (-0.5 / (unit * unit)),
            m_one,
        ]
        for h in range(3):
            values.append(tints[h, pl.ds(pl.multiple_of(i * 8, 8), 8), :])
        for f, value in enumerate(values):
            out_ref[pl.ds(i * (8 * feats) + f, 8, stride=feats), :] = value
        return carry

    lax.fori_loop(0, 8, finish, 0)
    store_colors.wait()
    for i in range(32):
        store(i).wait()


def image_kernel(weights, colors, image_ref):
    @pl.when(pl.program_id(0) == 0)
    def _():
        image_ref[...] = jnp.zeros_like(image_ref)

    for i in range(image_step):
        weight = weights[256 * i : 256 * i + 256, :]
        top = weight.astype(bf16)
        low = (weight - top.astype(f32)).astype(bf16)
        color = colors[96 * i : 96 * i + 96, :].astype(bf16)
        both = jnp.dot(color, top, preferred_element_type=f32)
        image = both[0:48] + both[48:96]
        image += jnp.dot(color[0:48], low, preferred_element_type=f32)
        for h in range(3):
            image_ref[h] += image[16 * h : 16 * h + 16]


def render(tile_plan, tile_lengths, arrived, cots):
    shape = jax.ShapeDtypeStruct
    hbm = pl.BlockSpec(memory_space=pltpu.HBM)
    return call(
        render_kernel,
        (
            shape((colors_at + 3072, 256), f32),
            shape((64 * feats, 128), f32),
        ),
        (tile_plan, tile_lengths, arrived, cots),
        [smem, smem, vmem, vmem],
        [
            pltpu.VMEM((8192, 256), f32),
            pltpu.VMEM((3072, 256), f32),
            pltpu.VMEM((512, 128), f32),
            pltpu.VMEM((8192, 256), f32),
            pltpu.VMEM((8192, 256), f32),
            pltpu.VMEM((512, 128), f32),
            pltpu.VMEM((3, 64, 128), f32),
            pltpu.SemaphoreType.DMA((33,)),
        ],
        52,
        (hbm, vmem),
    )


def compose(made):
    return pl.pallas_call(
        image_kernel,
        out_shape=jax.ShapeDtypeStruct((3, 16, 256), f32),
        grid=(32 // image_step,),
        in_specs=[
            pl.BlockSpec((256 * image_step, 256), lambda i: (i, 0)),
            pl.BlockSpec((96 * image_step, 256), lambda i: (i + colors_at // (96 * image_step), 0)),
        ],
        out_specs=pl.BlockSpec((3, 16, 256), lambda i: (0, 0, 0)),
        compiler_params=pltpu.CompilerParams(vmem_limit_bytes=60 * 1024 * 1024),
    )(made, made)


def source_views(refs):
    sources = []
    for low, high in zip(refs[0::2], refs[1::2]):
        line = low[feats * 32 : feats * 32 + 8, :]
        camera = [jnp.broadcast_to(line[:, i : i + 1], (8, 128)) for i in range(8)]
        sources.append(((low, high), view_values(camera)))
    return sources


def view_gradient(sources, spread, step):
    at = step * (8 * pitch)
    first = step < 4

    def param(p):
        return spread[pl.ds(at + p, 8, stride=pitch), :]

    center = [param(p) for p in range(3)]
    shaped = [[param(params_n + 3 * j + k) for k in range(3)] for j in range(3)]
    harmonics = [param(p) for p in range(11, params_n)]
    total = None
    for (low, high), view in sources:
        lines = [pl.ds(32 * f + 8 * (step & 3), 8) for f in range(feats)]
        rows = [jnp.where(first, low[line, :], high[line, :]) for line in lines]

        def one(center, shaped, harmonics, view=view):
            return project(center, shaped, harmonics, view)

        _, back = jax.vjp(one, center, shaped, harmonics)
        d_center, d_shaped, d_harmonics = back(rows[:5] + rows[6:])
        part = d_center + sum(d_shaped, []) + [rows[5]] + d_harmonics
        total = part if total is None else [x + y for x, y in zip(total, part)]
    return total


def first_kernel(spread, low_ref, high_ref, out_ref):
    sources = source_views([low_ref, high_ref])

    def step(i, carry):
        rows = pl.ds(pl.multiple_of(i * 8, 8), 8)
        for p, value in enumerate(view_gradient(sources, spread, i)):
            out_ref[p, rows, :] = value
        return carry

    lax.fori_loop(0, 8, step, 0)


def middle_kernel(spread, left_low, left_high, right_low, right_high, sum_ref, out_ref):
    sources = source_views([left_low, left_high, right_low, right_high])

    def step(i, carry):
        rows = pl.ds(pl.multiple_of(i * 8, 8), 8)
        for p, value in enumerate(view_gradient(sources, spread, i)):
            out_ref[p, rows, :] = value + sum_ref[p, rows, :]
        return carry

    lax.fori_loop(0, 8, step, 0)


def last_kernel(spread, low_ref, high_ref, sum_ref, out_hbm, held, out_ref, sems):
    sources = source_views([low_ref, high_ref])

    def copy(i):
        column = pl.ds(pl.multiple_of(i * 1024, 1024), 1024)
        return pltpu.make_async_copy(out_ref.at[:, column], out_hbm.at[:, column], sems.at[i])

    def step(i, carry):
        rows = pl.ds(pl.multiple_of(i * 8, 8), 8)
        total = view_gradient(sources, spread, i)
        total = [value + sum_ref[p, rows, :] for p, value in enumerate(total)]
        params = [spread[pl.ds(i * (8 * pitch) + p, 8, stride=pitch), :] for p in range(3, 11)]
        _, back = jax.vjp(lambda *p: shape_matrix(p), *params[:7])
        d_shape = back([total[3 + 3 * j : 6 + 3 * j] for j in range(3)])
        d_logit = total[12] / (1.0 + jnp.exp(params[7]))
        for p, value in enumerate(total[0:3] + list(d_shape) + [d_logit] + total[13:]):
            held[pl.ds(p, 8, stride=pitch), :] = value
        for tile in range(8):
            column = pl.ds(pl.multiple_of(i * 1024 + tile * 128, 128), 128)
            row = tile * pitch
            out_ref[0:56, column] = held[row : row + 56, :]
            out_ref[56:59, column] = held[row + 56 : row + 59, :]
        copy(i).start()
        return carry

    lax.fori_loop(0, 8, step, 0)
    for i in range(8):
        copy(i).wait()


def call(kernel, out, args, specs, scratch, limit=8, out_specs=None):
    return pl.pallas_call(
        kernel,
        out_shape=out,
        in_specs=specs,
        out_specs=out_specs or jax.tree.map(lambda _: vmem, out),
        scratch_shapes=scratch,
        compiler_params=pltpu.CompilerParams(vmem_limit_bytes=limit * 1024 * 1024),
    )(*args)


def exchange(rows, width):
    parts = rows.reshape(owners, width, 1, 128)
    parts = lax.all_to_all(parts, "space", split_axis=0, concat_axis=0, tiled=True)
    return parts.reshape(owners * width, 128)


def per_device(
    gaussians, camera_table, view_camera, tile_plan, requests, tile_lists, tile_lengths, pixel_grad
):
    shape = jax.ShapeDtypeStruct
    ordered = call(
        order_kernel,
        shape((64, 128), jnp.int32),
        (requests[0, 0], tile_lists[0]),
        [pl.BlockSpec(memory_space=pltpu.HBM)] * 2,
        [
            pltpu.VMEM((64, 128), jnp.int32),
            pltpu.VMEM((128, 512), jnp.int32),
            pltpu.VMEM((512, 128), jnp.int32),
            pltpu.SemaphoreType.DMA((2,)),
        ],
        60,
    )
    incoming = exchange(ordered, 1)
    table, spread = call(
        project_kernel,
        (
            shape(((2 * feats + 2) * 32, 256), bf16),
            shape((64 * pitch, 128), f32),
        ),
        (camera_table.T, view_camera, gaussians),
        [smem, smem, pl.BlockSpec(memory_space=pltpu.HBM)],
        [
            pltpu.VMEM((params_n, slots), f32),
            pltpu.VMEM((feats, 64, 128), f32),
            pltpu.SemaphoreType.DMA((8,)),
        ],
        16,
    )
    picked = pick(incoming, table)
    arrived = exchange(picked, feats)
    inverse = invert(incoming)
    made, row_grad = render(
        tile_plan, tile_lengths, arrived, jnp.transpose(pixel_grad[0], (1, 0, 2))
    )
    returned = exchange(row_grad, feats)
    image = compose(made)
    returned, image = lax.optimization_barrier((returned, image))
    low, high = place(camera_table.T, view_camera, inverse, returned)
    ahead = [(i, (i + 1) % 4) for i in range(4)]
    behind = [(i, (i - 1) % 4) for i in range(4)]
    left_low = lax.ppermute(low, "view", ahead)
    right_high = lax.ppermute(high, "view", behind)
    left_high = lax.ppermute(high, "view", ahead)
    right_low = lax.ppermute(low, "view", behind)
    part = shape((61, 64, 128), f32)
    total = call(first_kernel, part, (spread, low, high), [vmem] * 3, [], 12)
    left_low, right_high, total = lax.optimization_barrier((left_low, right_high, total))
    far_low = lax.ppermute(left_low, "view", ahead)
    far_high = lax.ppermute(right_high, "view", behind)
    total = call(
        middle_kernel,
        part,
        (spread, left_low, left_high, right_low, right_high, total),
        [vmem] * 6,
        [],
        16,
    )
    total = call(
        last_kernel,
        shape((params_n, slots), f32),
        (spread, far_low, far_high, total),
        [vmem] * 4,
        [
            pltpu.VMEM((8 * pitch, 128), f32),
            pltpu.VMEM((params_n, slots), f32),
            pltpu.SemaphoreType.DMA((8,)),
        ],
        16,
        pl.BlockSpec(memory_space=pltpu.HBM),
    )
    return (jnp.transpose(image, (1, 0, 2))[None], total)


def solution(mesh):
    placed = (
        P(None, "space"),
        P(),
        P("view"),
        P("view", "space"),
        P("view", "space", None, None),
        P("view", "space", None),
        P("view", "space"),
        P("view", "space", None, None),
    )
    return jax.shard_map(
        per_device,
        mesh=mesh,
        in_specs=placed,
        out_specs=(P("view", "space", None, None), P(None, "space")),
        check_vma=False,
    )
```

```python
import jax
import jax.numpy as jnp
from jax import lax
from jax.experimental import pallas as pl
from jax.experimental.pallas import tpu as pltpu
from jax.sharding import PartitionSpec as P

sh_zero = 0.28209479177387814
sh_one = 0.4886025119029199
sh_two = (
    1.0925484305920792,
    -1.0925484305920792,
    0.31539156525252005,
    -1.0925484305920792,
    0.5462742152960396,
)
sh_three = (
    -0.5900435899266435,
    2.890611442640554,
    -0.4570457994644658,
    0.3731763325901154,
    -0.4570457994644658,
    1.445305721320277,
    -0.5900435899266435,
)
dilation = 0.3 / 291600.0
log2e = 1.4426950408889634
unit = 1080.0
params_n = 59
feats = 9
owners = 64
slots = 8192
pitch = 72
half_rows = 296
lay_unroll = 16
image_step = 8
colors_at = 8448
forward_unroll = 16
backward_unroll = 16
pick_unroll = 16
vmem = pl.BlockSpec(memory_space=pltpu.VMEM)
smem = pl.BlockSpec(memory_space=pltpu.SMEM)
f32 = jnp.float32
bf16 = jnp.bfloat16


def quat_matrix(quat_w, quat_x, quat_y, quat_z):
    inv = 1.0 / jnp.sqrt(
        quat_w * quat_w + quat_x * quat_x + quat_y * quat_y + quat_z * quat_z
    )
    unit_w = quat_w * inv
    unit_x = quat_x * inv
    unit_y = quat_y * inv
    unit_z = quat_z * inv
    return [
        [
            1.0 - 2.0 * (unit_y * unit_y + unit_z * unit_z),
            2.0 * (unit_x * unit_y - unit_w * unit_z),
            2.0 * (unit_x * unit_z + unit_w * unit_y),
        ],
        [
            2.0 * (unit_x * unit_y + unit_w * unit_z),
            1.0 - 2.0 * (unit_x * unit_x + unit_z * unit_z),
            2.0 * (unit_y * unit_z - unit_w * unit_x),
        ],
        [
            2.0 * (unit_x * unit_z - unit_w * unit_y),
            2.0 * (unit_y * unit_z + unit_w * unit_x),
            1.0 - 2.0 * (unit_x * unit_x + unit_y * unit_y),
        ],
    ]


def sh_basis(dir_x, dir_y, dir_z):
    sq_x = dir_x * dir_x
    sq_y = dir_y * dir_y
    sq_z = dir_z * dir_z
    return [
        sh_zero,
        -sh_one * dir_y,
        sh_one * dir_z,
        -sh_one * dir_x,
        sh_two[0] * dir_x * dir_y,
        sh_two[1] * dir_y * dir_z,
        sh_two[2] * (2.0 * sq_z - sq_x - sq_y),
        sh_two[3] * dir_x * dir_z,
        sh_two[4] * (sq_x - sq_y),
        sh_three[0] * dir_y * (3.0 * sq_x - sq_y),
        sh_three[1] * dir_x * dir_y * dir_z,
        sh_three[2] * dir_y * (4.0 * sq_z - sq_x - sq_y),
        sh_three[3] * dir_z * (2.0 * sq_z - 3.0 * sq_x - 3.0 * sq_y),
        sh_three[4] * dir_x * (4.0 * sq_z - sq_x - sq_y),
        sh_three[5] * dir_z * (sq_x - sq_y),
        sh_three[6] * dir_x * (sq_x - 3.0 * sq_y),
    ]


def shape_matrix(params):
    scales = [jnp.exp(params[0]), jnp.exp(params[1]), jnp.exp(params[2])]
    own_rot = quat_matrix(params[3], params[4], params[5], params[6])
    return [[own_rot[i][k] * scales[k] for k in range(3)] for i in range(3)]


def view_values(camera):
    view_rot = quat_matrix(camera[0], camera[1], camera[2], camera[3])
    offset_cam = [camera[4], camera[5], camera[6]]
    back = [sum(view_rot[j][i] * offset_cam[j] for j in range(3)) for i in range(3)]
    return view_rot, offset_cam, camera[7], back


def project(center, shaped, harmonics, view):
    view_rot, offset_cam, focal_len, back = view
    in_camera = [
        sum(view_rot[i][j] * center[j] for j in range(3)) + offset_cam[i] for i in range(3)
    ]
    turned = [
        [sum(view_rot[i][j] * shaped[j][k] for j in range(3)) for k in range(3)] for i in range(3)
    ]
    inv_depth = 1.0 / in_camera[2]
    near = focal_len * inv_depth
    screen_u = near * in_camera[0]
    screen_v = near * in_camera[1]
    slope_u = screen_u * inv_depth
    slope_v = screen_v * inv_depth
    jac_u = [near * turned[0][k] - slope_u * turned[2][k] for k in range(3)]
    jac_v = [near * turned[1][k] - slope_v * turned[2][k] for k in range(3)]
    cov_uu = sum(jac_u[k] * jac_u[k] for k in range(3)) + dilation
    cov_uv = sum(jac_u[k] * jac_v[k] for k in range(3))
    cov_vv = sum(jac_v[k] * jac_v[k] for k in range(3)) + dilation
    inv_det = 1.0 / (cov_uu * cov_vv - cov_uv * cov_uv)
    toward = [center[i] + back[i] for i in range(3)]
    inv_len = 1.0 / jnp.sqrt(
        toward[0] * toward[0] + toward[1] * toward[1] + toward[2] * toward[2]
    )
    basis = sh_basis(toward[0] * inv_len, toward[1] * inv_len, toward[2] * inv_len)
    colors = [0.5 + sum(basis[k] * harmonics[3 * k + h] for k in range(16)) for h in range(3)]
    return [
        screen_u,
        screen_v,
        cov_vv * inv_det,
        -cov_uv * inv_det,
        cov_uu * inv_det,
    ] + colors


def log_opacity(logit):
    return jnp.minimum(logit, 0.0) - jnp.log1p(jnp.exp(-jnp.abs(logit)))


def pieces(value, count):
    out = []
    for _ in range(count - 1):
        top = value.astype(bf16).astype(f32)
        out.append(top)
        value = value - top
    out.append(value.astype(bf16).astype(f32))
    return out


def iota(shape, axis):
    return lax.broadcasted_iota(jnp.int32, shape, axis)


def order_kernel(requests_hbm, lists_hbm, out_ref, requests, lists, turned, sems):
    copies = [
        pltpu.make_async_copy(lists_hbm, lists, sems.at[0]),
        pltpu.make_async_copy(requests_hbm, requests, sems.at[1]),
    ]
    for copy in copies:
        copy.start()
    for copy in copies:
        copy.wait()
    turned[:, 0:16] = lists[...].T
    group = iota((64, 128), 1) // 16
    entry = jnp.zeros((64, 128), jnp.int32)
    for j in range(8):
        piece = turned[pl.ds(j, 64, stride=8), :]
        if j:
            piece = pltpu.roll(piece, 16 * j, 1)
        entry = jnp.where(group == j, piece, entry)
    out_ref[...] = jnp.take_along_axis(requests[...], entry & 127, axis=1)


def camera_values(table_ref, view_ref):
    row = view_ref[0]
    return [jnp.full((8, 128), table_ref[i, row], f32) for i in range(8)]


def tile_frame(plan_ref, length_ref):
    lane_tile = iota((8, 128), 1) & 15
    center_u = jnp.zeros((8, 128), f32)
    center_v = jnp.zeros((8, 128), f32)
    length = jnp.zeros((8, 128), jnp.int32)
    for t in range(16):
        tile = plan_ref[0, t]
        down = tile // 120
        across = tile - down * 120
        at_u = (across * 16 + 8 - 960).astype(f32)
        at_v = (down * 16 + 8 - 540).astype(f32)
        center_u = jnp.where(lane_tile == t, at_u, center_u)
        center_v = jnp.where(lane_tile == t, at_v, center_v)
        length = jnp.where(lane_tile == t, length_ref[0, t], length)
    return center_u / 540.0, center_v / 540.0, length


def project_kernel(
    table_ref, view_ref, gauss_hbm, out_ref, spread, gauss, held, sems
):
    def fetch(i):
        column = pl.ds(pl.multiple_of(i * 1024, 1024), 1024)
        return pltpu.make_async_copy(gauss_hbm.at[:, column], gauss.at[:, column], sems.at[i])

    for i in range(8):
        fetch(i).start()
    view = view_values(camera_values(table_ref, view_ref))

    def step(i, carry):
        at = i * (8 * pitch)
        fetch(i).wait()
        for tile in range(8):
            column = pl.ds(pl.multiple_of(i * 1024 + tile * 128, 128), 128)
            row = pl.multiple_of(at + tile * pitch, 8)
            spread[pl.ds(row, 56), :] = gauss[0:56, column]
            spread[pl.ds(row + 56, 3), :] = gauss[56:59, column]
        params = [spread[pl.ds(at + p, 8, stride=pitch), :] for p in range(params_n)]
        shaped = shape_matrix(params[3:10])
        for k in range(9):
            spread[pl.ds(at + params_n + k, 8, stride=pitch), :] = shaped[k // 3][k % 3]
        out = project(params[0:3], shaped, params[11:], view)
        out = out[:5] + [log_opacity(params[10])] + out[5:]
        for f in range(feats):
            held[f, pl.ds(pl.multiple_of(i * 8, 8), 8), :] = out[f]
        return carry

    lax.fori_loop(0, 8, step, 0)
    for f in range(feats):
        for part, value in enumerate(pieces(held[f], 3 if f < 2 else 2)):
            row = (part * feats + f) * 32
            out_ref[row : row + 32, 0:128] = value[0:32].astype(bf16)
            out_ref[row : row + 32, 128:256] = value[32:64].astype(bf16)


def slot_hot(index):
    place = (index >> 12) * 128 + (index & 127)
    return (iota((256, index.shape[1]), 0) == place).astype(f32).astype(bf16)


def pick_rows(index_ref, table_ref, held, third):
    rows = feats * 32

    def step(pair, carry):
        index = jnp.concatenate(
            [index_ref[pl.ds(2 * pair, 1), :], index_ref[pl.ds(2 * pair + 1, 1), :]], axis=1
        )
        got = jnp.dot(table_ref[...], slot_hot(index), preferred_element_type=f32)
        level = (index >> 7) & 31
        keep = iota((32, 256), 0) == level
        for f in range(feats):
            value = got[32 * f : 32 * f + 32] + got[rows + 32 * f : rows + 32 * f + 32]
            if f < third:
                value += got[2 * rows + 32 * f : 2 * rows + 32 * f + 32]
            value = jnp.sum(jnp.where(keep, value, 0.0), axis=0, keepdims=True)
            held(f, 2 * pair, value[:, 0:128])
            held(f, 2 * pair + 1, value[:, 128:256])
        return carry

    lax.fori_loop(0, index_ref.shape[0] // 2, step, 0, unroll=pick_unroll)


def pick_kernel(index_ref, table_ref, out_ref, held):
    def keep(f, row, value):
        held[f, pl.ds(row, 1), :] = value

    pick_rows(index_ref, table_ref, keep, 2)
    for f in range(feats):
        out_ref[pl.ds(f, 64, stride=feats), :] = held[f]


def inverse_kernel(index_ref, low_ref, high_ref, total):
    total[...] = jnp.zeros_like(total)

    def step(pair, carry):
        index = jnp.concatenate(
            [index_ref[pl.ds(2 * pair, 1), :], index_ref[pl.ds(2 * pair + 1, 1), :]], axis=1
        )
        keep = iota((32, 256), 0) == ((index >> 7) & 31)
        lane = iota((32, 256), 1)
        row = (2 * pair + (lane >> 7)).astype(f32)
        column = (lane & 127).astype(f32)
        both = jnp.concatenate([jnp.where(keep, row, 0.0), jnp.where(keep, column, 0.0)], axis=0)
        total[...] += lax.dot_general(
            both.astype(bf16),
            slot_hot(index),
            (((1,), (1,)), ((), ())),
            preferred_element_type=f32,
        )
        return carry

    lax.fori_loop(0, 32, step, 0, unroll=4)
    spot = (total[0:32] * 128.0 + total[32:64]).astype(jnp.int32)
    low_ref[...] = spot[:, 0:128]
    high_ref[...] = spot[:, 128:256]


def place_kernel(camera_ref, view_ref, index_ref, grad_ref, out_ref, table):
    for f in range(feats):
        value = grad_ref[pl.ds(f, 64, stride=feats), :]
        for part, piece in enumerate(pieces(value, 2)):
            row = (part * feats + f) * 32
            table[row : row + 32, 0:128] = piece[0:32].astype(bf16)
            table[row : row + 32, 128:256] = piece[32:64].astype(bf16)
    lane = iota((8, 128), 1)
    camera = jnp.zeros((8, 128), f32)
    for i in range(8):
        camera = jnp.where(lane == i, camera_ref[i, view_ref[0]], camera)
    out_ref[feats * 32 :, :] = camera

    def keep(f, row, value):
        out_ref[pl.ds(f * 32 + row, 1), :] = value

    pick_rows(index_ref, table, keep, 0)


def pick(incoming, table):
    return call(
        pick_kernel,
        jax.ShapeDtypeStruct((64 * feats, 128), f32),
        (incoming, table),
        [vmem, vmem],
        [pltpu.VMEM((feats, 64, 128), f32)],
    )


def invert(incoming):
    half = jax.ShapeDtypeStruct((32, 128), jnp.int32)
    return call(
        inverse_kernel,
        (half, half),
        (incoming,),
        [vmem],
        [pltpu.VMEM((64, 256), f32)],
    )


def place(camera_table, view_camera, inverse, returned):
    return call(
        place_kernel,
        jax.ShapeDtypeStruct((half_rows, 128), f32),
        (camera_table, view_camera, inverse, returned),
        [smem, smem, vmem, vmem],
        [pltpu.VMEM((2 * feats * 32, 256), bf16)],
    )


def render_kernel(
    plan_ref,
    length_ref,
    rows_ref,
    cot_ref,
    made_hbm,
    out_ref,
    weights,
    colors,
    coef,
    alphas,
    shades,
    moments,
    tints,
    sems,
):
    lane_step = iota((8, 128), 1) >> 4
    center_u, center_v, length = tile_frame(plan_ref, length_ref)

    def feature(i, f):
        return rows_ref[pl.ds(i * (8 * feats) + f, 8, stride=feats), :]

    coef[...] = jnp.zeros_like(coef)

    def prepare(i, carry):
        off_u = (feature(i, 0) - center_u) * unit
        off_v = (feature(i, 1) - center_v) * unit
        quad_u = feature(i, 2) * (-0.5 * log2e / (unit * unit))
        quad_m = feature(i, 3) * (-log2e / (unit * unit))
        quad_v = feature(i, 4) * (-0.5 * log2e / (unit * unit))
        lead = quad_u * off_u + quad_m * off_v
        base = off_u * lead + quad_v * off_v * off_v + feature(i, 5) * log2e
        alive = (iota((8, 128), 0) + 8 * i) * 8 + lane_step < length
        values = [
            jnp.where(alive, base, -30000.0),
            jnp.where(alive, -(lead + quad_u * off_u), 0.0),
            jnp.where(alive, -(2.0 * quad_v * off_v + quad_m * off_u), 0.0),
            jnp.where(alive, quad_u, 0.0),
            jnp.where(alive, quad_m, 0.0),
            jnp.where(alive, quad_v, 0.0),
        ]
        for m, value in enumerate(values):
            coef[pl.ds(i * 64 + m, 8, stride=8), :] = value
        return carry

    lax.fori_loop(0, 8, prepare, 0)

    def monomials(shape):
        row = iota(shape, 0) & 7
        pixel = iota(shape, 1)
        at_x = ((pixel & 15) * 2 - 15).astype(f32)
        at_y = ((pixel >> 4) * 2 - 15).astype(f32)
        out = jnp.where(row == 0, 1.0, 0.0)
        out = jnp.where(row == 1, at_x, out)
        out = jnp.where(row == 2, at_y, out)
        out = jnp.where(row == 3, at_x * at_x, out)
        out = jnp.where(row == 4, at_x * at_y, out)
        return jnp.where(row == 5, at_y * at_y, out)

    terms = jnp.where(iota((32, 256), 0) < 24, monomials((32, 256)), 0.0).astype(bf16)
    moment_terms = monomials((16, 256)).astype(bf16)
    cot_parts = [pieces(cot_ref[h], 2) for h in range(3)]
    cot_high = jnp.concatenate([p[0] for p in cot_parts], axis=0).astype(bf16)
    cot_low = jnp.concatenate([p[1] for p in cot_parts], axis=0).astype(bf16)
    cot_both = jnp.concatenate([cot_high, cot_low], axis=0)
    cot_all = jnp.concatenate([cot_high, cot_high, cot_low], axis=0)
    same_tile = (iota((48, 256), 0) & 15) == (iota((48, 256), 1) & 15)
    own_tile = iota((16, 256), 0) == (iota((16, 256), 1) & 15)
    across = (((1,), (1,)), ((), ()))
    along = (((0,), (0,)), ((), ()))

    def pair(i, ref, row, step):
        return jnp.concatenate(
            [ref[pl.ds(2 * i * step + row, 1), :], ref[pl.ds((2 * i + 1) * step + row, 1), :]],
            axis=1,
        )

    def lay(i, carry):
        raw = jnp.concatenate(
            [
                coef[pl.ds(pl.multiple_of(i * 16, 8), 8), :],
                coef[pl.ds(pl.multiple_of(i * 16 + 8, 8), 8), :],
            ],
            axis=1,
        )
        block = jnp.concatenate(pieces(raw, 3) + [jnp.zeros((8, 256), f32)], axis=0)
        base = pl.multiple_of(i * 256, 256)
        power = lax.dot_general(
            block.astype(bf16), terms, along, preferred_element_type=f32
        )
        alphas[pl.ds(base, 256), :] = jnp.exp2(power)
        high = []
        low = []
        for h in range(3):
            value = jnp.where(own_tile, pair(i, rows_ref, 6 + h, feats), 0.0)
            parts = pieces(value, 2)
            high.append(parts[0])
            low.append(parts[1])
        color = jnp.concatenate(high + low, axis=0)
        colors[pl.ds(pl.multiple_of(i * 96, 8), 96), :] = color
        color = jnp.concatenate([color] + high, axis=0).astype(bf16)
        shades[pl.ds(base, 256), :] = lax.dot_general(
            color, cot_all, along, preferred_element_type=f32
        )
        return carry

    lax.fori_loop(0, 32, lay, 0, unroll=lay_unroll)

    def store(i):
        rows = pl.ds(pl.multiple_of(i * 256, 256), 256)
        return pltpu.make_async_copy(weights.at[rows], made_hbm.at[rows], sems.at[i])

    store_colors = pltpu.make_async_copy(colors, made_hbm.at[colors_at : colors_at + 3072], sems.at[32])
    store_colors.start()

    def forward(i, clear):
        base = pl.multiple_of(i * 256, 256)
        kept = []
        for k in range(16):
            weight = alphas[pl.ds(base + 16 * k, 16), :] * clear
            clear = clear - weight
            kept.append(weight)
        weight = jnp.concatenate(kept, axis=0)
        weights[pl.ds(base, 256), :] = weight
        store(i).start()
        top = weight.astype(bf16)
        low = (weight - top.astype(f32)).astype(bf16)
        both = lax.dot_general(cot_both, top, across, preferred_element_type=f32)
        tint = both[0:48] + both[48:96]
        tint += lax.dot_general(cot_high, low, across, preferred_element_type=f32)
        tint = jnp.where(same_tile, tint, 0.0)
        for h in range(3):
            value = jnp.sum(tint[16 * h : 16 * h + 16], axis=0, keepdims=True)
            for own in range(2):
                tints[h, pl.ds(2 * i + own, 1), :] = value[:, 128 * own : 128 * own + 128]
        return clear

    lax.fori_loop(0, 32, forward, jnp.ones((16, 256), f32), unroll=forward_unroll)

    def backward(step, behind):
        i = 31 - step
        base = pl.multiple_of(i * 256, 256)
        kept = [None] * 16
        for k in range(15, -1, -1):
            rows = pl.ds(base + 16 * k, 16)
            alpha = alphas[rows, :]
            shown = shades[rows, :]
            kept[k] = weights[rows, :] * (shown - behind)
            behind = (1.0 - alpha) * behind + alpha * shown
        slope = jnp.concatenate(kept, axis=0)
        top = slope.astype(bf16)
        low = (slope - top.astype(f32)).astype(bf16)
        moment = lax.dot_general(moment_terms, top, across, preferred_element_type=f32)
        moment += lax.dot_general(moment_terms, low, across, preferred_element_type=f32)
        for own in range(2):
            moments[pl.ds(pl.multiple_of(i * 16 + own * 8, 8), 8), :] = moment[
                0:8, 128 * own : 128 * own + 128
            ]
        return behind

    lax.fori_loop(0, 32, backward, jnp.zeros((16, 256), f32), unroll=backward_unroll)

    def finish(i, carry):
        off_u = (feature(i, 0) - center_u) * unit
        off_v = (feature(i, 1) - center_v) * unit
        m_one, m_x, m_y, m_xx, m_xy, m_yy = [
            moments[pl.ds(i * 64 + m, 8, stride=8), :] for m in range(6)
        ]
        n_x = m_x - off_u * m_one
        n_y = m_y - off_v * m_one
        n_xx = m_xx - off_u * (m_x + n_x)
        n_xy = m_xy - off_u * m_y - off_v * n_x
        n_yy = m_yy - off_v * (m_y + n_y)
        values = [
            (feature(i, 2) * n_x + feature(i, 3) * n_y) * (1.0 / unit),
            (feature(i, 3) * n_x + feature(i, 4) * n_y) * (1.0 / unit),
            n_xx * (-0.5 / (unit * unit)),
            n_xy * (-1.0 / (unit * unit)),
            n_yy * (-0.5 / (unit * unit)),
            m_one,
        ]
        for h in range(3):
            values.append(tints[h, pl.ds(pl.multiple_of(i * 8, 8), 8), :])
        for f, value in enumerate(values):
            out_ref[pl.ds(i * (8 * feats) + f, 8, stride=feats), :] = value
        return carry

    lax.fori_loop(0, 8, finish, 0)
    store_colors.wait()
    for i in range(32):
        store(i).wait()


def image_kernel(weights, colors, image_ref):
    @pl.when(pl.program_id(0) == 0)
    def _():
        image_ref[...] = jnp.zeros_like(image_ref)

    for i in range(image_step):
        weight = weights[256 * i : 256 * i + 256, :]
        top = weight.astype(bf16)
        low = (weight - top.astype(f32)).astype(bf16)
        color = colors[96 * i : 96 * i + 96, :].astype(bf16)
        both = jnp.dot(color, top, preferred_element_type=f32)
        image = both[0:48] + both[48:96]
        image += jnp.dot(color[0:48], low, preferred_element_type=f32)
        for h in range(3):
            image_ref[h] += image[16 * h : 16 * h + 16]


def render(tile_plan, tile_lengths, arrived, cots):
    shape = jax.ShapeDtypeStruct
    hbm = pl.BlockSpec(memory_space=pltpu.HBM)
    return call(
        render_kernel,
        (
            shape((colors_at + 3072, 256), f32),
            shape((64 * feats, 128), f32),
        ),
        (tile_plan, tile_lengths, arrived, cots),
        [smem, smem, vmem, vmem],
        [
            pltpu.VMEM((8192, 256), f32),
            pltpu.VMEM((3072, 256), f32),
            pltpu.VMEM((512, 128), f32),
            pltpu.VMEM((8192, 256), f32),
            pltpu.VMEM((8192, 256), f32),
            pltpu.VMEM((512, 128), f32),
            pltpu.VMEM((3, 64, 128), f32),
            pltpu.SemaphoreType.DMA((33,)),
        ],
        52,
        (hbm, vmem),
    )


def compose(made):
    return pl.pallas_call(
        image_kernel,
        out_shape=jax.ShapeDtypeStruct((3, 16, 256), f32),
        grid=(32 // image_step,),
        in_specs=[
            pl.BlockSpec((256 * image_step, 256), lambda i: (i, 0)),
            pl.BlockSpec((96 * image_step, 256), lambda i: (i + colors_at // (96 * image_step), 0)),
        ],
        out_specs=pl.BlockSpec((3, 16, 256), lambda i: (0, 0, 0)),
        compiler_params=pltpu.CompilerParams(vmem_limit_bytes=60 * 1024 * 1024),
    )(made, made)


def source_views(refs):
    sources = []
    for low, high in zip(refs[0::2], refs[1::2]):
        line = low[feats * 32 : feats * 32 + 8, :]
        camera = [jnp.broadcast_to(line[:, i : i + 1], (8, 128)) for i in range(8)]
        sources.append(((low, high), view_values(camera)))
    return sources


def view_gradient(sources, spread, step):
    at = step * (8 * pitch)
    first = step < 4

    def param(p):
        return spread[pl.ds(at + p, 8, stride=pitch), :]

    center = [param(p) for p in range(3)]
    shaped = [[param(params_n + 3 * j + k) for k in range(3)] for j in range(3)]
    harmonics = [param(p) for p in range(11, params_n)]
    total = None
    for (low, high), view in sources:
        lines = [pl.ds(32 * f + 8 * (step & 3), 8) for f in range(feats)]
        rows = [jnp.where(first, low[line, :], high[line, :]) for line in lines]

        def one(center, shaped, harmonics, view=view):
            return project(center, shaped, harmonics, view)

        _, back = jax.vjp(one, center, shaped, harmonics)
        d_center, d_shaped, d_harmonics = back(rows[:5] + rows[6:])
        part = d_center + sum(d_shaped, []) + [rows[5]] + d_harmonics
        total = part if total is None else [x + y for x, y in zip(total, part)]
    return total


def first_kernel(spread, low_ref, high_ref, out_ref):
    sources = source_views([low_ref, high_ref])

    def step(i, carry):
        rows = pl.ds(pl.multiple_of(i * 8, 8), 8)
        for p, value in enumerate(view_gradient(sources, spread, i)):
            out_ref[p, rows, :] = value
        return carry

    lax.fori_loop(0, 8, step, 0)


def middle_kernel(spread, left_low, left_high, right_low, right_high, sum_ref, out_ref):
    sources = source_views([left_low, left_high, right_low, right_high])

    def step(i, carry):
        rows = pl.ds(pl.multiple_of(i * 8, 8), 8)
        for p, value in enumerate(view_gradient(sources, spread, i)):
            out_ref[p, rows, :] = value + sum_ref[p, rows, :]
        return carry

    lax.fori_loop(0, 8, step, 0)


def last_kernel(spread, low_ref, high_ref, sum_ref, out_hbm, held, out_ref, sems):
    sources = source_views([low_ref, high_ref])

    def copy(i):
        column = pl.ds(pl.multiple_of(i * 1024, 1024), 1024)
        return pltpu.make_async_copy(out_ref.at[:, column], out_hbm.at[:, column], sems.at[i])

    def step(i, carry):
        rows = pl.ds(pl.multiple_of(i * 8, 8), 8)
        total = view_gradient(sources, spread, i)
        total = [value + sum_ref[p, rows, :] for p, value in enumerate(total)]
        params = [spread[pl.ds(i * (8 * pitch) + p, 8, stride=pitch), :] for p in range(3, 11)]
        _, back = jax.vjp(lambda *p: shape_matrix(p), *params[:7])
        d_shape = back([total[3 + 3 * j : 6 + 3 * j] for j in range(3)])
        d_logit = total[12] / (1.0 + jnp.exp(params[7]))
        for p, value in enumerate(total[0:3] + list(d_shape) + [d_logit] + total[13:]):
            held[pl.ds(p, 8, stride=pitch), :] = value
        for tile in range(8):
            column = pl.ds(pl.multiple_of(i * 1024 + tile * 128, 128), 128)
            row = tile * pitch
            out_ref[0:56, column] = held[row : row + 56, :]
            out_ref[56:59, column] = held[row + 56 : row + 59, :]
        copy(i).start()
        return carry

    lax.fori_loop(0, 8, step, 0)
    for i in range(8):
        copy(i).wait()


def call(kernel, out, args, specs, scratch, limit=8, out_specs=None):
    return pl.pallas_call(
        kernel,
        out_shape=out,
        in_specs=specs,
        out_specs=out_specs or jax.tree.map(lambda _: vmem, out),
        scratch_shapes=scratch,
        compiler_params=pltpu.CompilerParams(vmem_limit_bytes=limit * 1024 * 1024),
    )(*args)


def exchange(rows, width):
    parts = rows.reshape(owners, width, 1, 128)
    parts = lax.all_to_all(parts, "space", split_axis=0, concat_axis=0, tiled=True)
    return parts.reshape(owners * width, 128)


def per_device(
    gaussians, camera_table, view_camera, tile_plan, requests, tile_lists, tile_lengths, pixel_grad
):
    shape = jax.ShapeDtypeStruct
    ordered = call(
        order_kernel,
        shape((64, 128), jnp.int32),
        (requests[0, 0], tile_lists[0]),
        [pl.BlockSpec(memory_space=pltpu.HBM)] * 2,
        [
            pltpu.VMEM((64, 128), jnp.int32),
            pltpu.VMEM((16, 512), jnp.int32),
            pltpu.VMEM((512, 128), jnp.int32),
            pltpu.SemaphoreType.DMA((2,)),
        ],
        60,
    )
    incoming = exchange(ordered, 1)
    table, spread = call(
        project_kernel,
        (
            shape(((2 * feats + 2) * 32, 256), bf16),
            shape((64 * pitch, 128), f32),
        ),
        (camera_table.T, view_camera, gaussians),
        [smem, smem, pl.BlockSpec(memory_space=pltpu.HBM)],
        [
            pltpu.VMEM((params_n, slots), f32),
            pltpu.VMEM((feats, 64, 128), f32),
            pltpu.SemaphoreType.DMA((8,)),
        ],
        16,
    )
    picked = pick(incoming, table)
    arrived = exchange(picked, feats)
    inverse_low, inverse_high = invert(incoming)
    made, row_grad = render(
        tile_plan, tile_lengths, arrived, jnp.transpose(pixel_grad[0], (1, 0, 2))
    )
    returned = exchange(row_grad, feats)
    image = compose(made)
    returned, image = lax.optimization_barrier((returned, image))
    low = place(camera_table.T, view_camera, inverse_low, returned)
    ahead = [(i, (i + 1) % 4) for i in range(4)]
    behind = [(i, (i - 1) % 4) for i in range(4)]
    left_low = lax.ppermute(low, "view", ahead)
    right_low = lax.ppermute(low, "view", behind)
    high = place(camera_table.T, view_camera, inverse_high, returned)
    right_high = lax.ppermute(high, "view", behind)
    left_high = lax.ppermute(high, "view", ahead)
    part = shape((61, 64, 128), f32)
    total = call(first_kernel, part, (spread, low, high), [vmem] * 3, [], 12)
    left_low, right_high, total = lax.optimization_barrier((left_low, right_high, total))
    far_low = lax.ppermute(left_low, "view", ahead)
    far_high = lax.ppermute(right_high, "view", behind)
    total = call(
        middle_kernel,
        part,
        (spread, left_low, left_high, right_low, right_high, total),
        [vmem] * 6,
        [],
        16,
    )
    total = call(
        last_kernel,
        shape((params_n, slots), f32),
        (spread, far_low, far_high, total),
        [vmem] * 4,
        [
            pltpu.VMEM((8 * pitch, 128), f32),
            pltpu.VMEM((params_n, slots), f32),
            pltpu.SemaphoreType.DMA((8,)),
        ],
        16,
        pl.BlockSpec(memory_space=pltpu.HBM),
    )
    return (jnp.transpose(image, (1, 0, 2))[None], total)


def solution(mesh):
    placed = (
        P(None, "space"),
        P(),
        P("view"),
        P("view", "space"),
        P("view", "space", None, None),
        P("view", "space", None),
        P("view", "space"),
        P("view", "space", None, None),
    )
    return jax.shard_map(
        per_device,
        mesh=mesh,
        in_specs=placed,
        out_specs=(P("view", "space", None, None), P(None, "space")),
        check_vma=False,
    )
```

```python
import jax
import jax.numpy as jnp
from jax import lax
from jax.experimental import pallas as pl
from jax.experimental.pallas import tpu as pltpu
from jax.sharding import PartitionSpec as P

sh_zero = 0.28209479177387814
sh_one = 0.4886025119029199
sh_two = (
    1.0925484305920792,
    -1.0925484305920792,
    0.31539156525252005,
    -1.0925484305920792,
    0.5462742152960396,
)
sh_three = (
    -0.5900435899266435,
    2.890611442640554,
    -0.4570457994644658,
    0.3731763325901154,
    -0.4570457994644658,
    1.445305721320277,
    -0.5900435899266435,
)
dilation = 0.3 / 291600.0
log2e = 1.4426950408889634
unit = 1080.0
params_n = 59
feats = 9
owners = 64
slots = 8192
pitch = 72
half_rows = 296
lay_unroll = 16
image_step = 8
features_at = 9216
forward_unroll = 32
backward_unroll = 32
pick_unroll = 16
vmem = pl.BlockSpec(memory_space=pltpu.VMEM)
smem = pl.BlockSpec(memory_space=pltpu.SMEM)
f32 = jnp.float32
bf16 = jnp.bfloat16


def quat_matrix(quat_w, quat_x, quat_y, quat_z):
    inv = 1.0 / jnp.sqrt(
        quat_w * quat_w + quat_x * quat_x + quat_y * quat_y + quat_z * quat_z
    )
    unit_w = quat_w * inv
    unit_x = quat_x * inv
    unit_y = quat_y * inv
    unit_z = quat_z * inv
    return [
        [
            1.0 - 2.0 * (unit_y * unit_y + unit_z * unit_z),
            2.0 * (unit_x * unit_y - unit_w * unit_z),
            2.0 * (unit_x * unit_z + unit_w * unit_y),
        ],
        [
            2.0 * (unit_x * unit_y + unit_w * unit_z),
            1.0 - 2.0 * (unit_x * unit_x + unit_z * unit_z),
            2.0 * (unit_y * unit_z - unit_w * unit_x),
        ],
        [
            2.0 * (unit_x * unit_z - unit_w * unit_y),
            2.0 * (unit_y * unit_z + unit_w * unit_x),
            1.0 - 2.0 * (unit_x * unit_x + unit_y * unit_y),
        ],
    ]


def sh_basis(dir_x, dir_y, dir_z):
    sq_x = dir_x * dir_x
    sq_y = dir_y * dir_y
    sq_z = dir_z * dir_z
    return [
        sh_zero,
        -sh_one * dir_y,
        sh_one * dir_z,
        -sh_one * dir_x,
        sh_two[0] * dir_x * dir_y,
        sh_two[1] * dir_y * dir_z,
        sh_two[2] * (2.0 * sq_z - sq_x - sq_y),
        sh_two[3] * dir_x * dir_z,
        sh_two[4] * (sq_x - sq_y),
        sh_three[0] * dir_y * (3.0 * sq_x - sq_y),
        sh_three[1] * dir_x * dir_y * dir_z,
        sh_three[2] * dir_y * (4.0 * sq_z - sq_x - sq_y),
        sh_three[3] * dir_z * (2.0 * sq_z - 3.0 * sq_x - 3.0 * sq_y),
        sh_three[4] * dir_x * (4.0 * sq_z - sq_x - sq_y),
        sh_three[5] * dir_z * (sq_x - sq_y),
        sh_three[6] * dir_x * (sq_x - 3.0 * sq_y),
    ]


def shape_matrix(params):
    scales = [jnp.exp(params[0]), jnp.exp(params[1]), jnp.exp(params[2])]
    own_rot = quat_matrix(params[3], params[4], params[5], params[6])
    return [[own_rot[i][k] * scales[k] for k in range(3)] for i in range(3)]


def view_values(camera):
    view_rot = quat_matrix(camera[0], camera[1], camera[2], camera[3])
    offset_cam = [camera[4], camera[5], camera[6]]
    back = [sum(view_rot[j][i] * offset_cam[j] for j in range(3)) for i in range(3)]
    return view_rot, offset_cam, camera[7], back


def project(center, shaped, harmonics, view):
    view_rot, offset_cam, focal_len, back = view
    in_camera = [
        sum(view_rot[i][j] * center[j] for j in range(3)) + offset_cam[i] for i in range(3)
    ]
    turned = [
        [sum(view_rot[i][j] * shaped[j][k] for j in range(3)) for k in range(3)] for i in range(3)
    ]
    inv_depth = 1.0 / in_camera[2]
    near = focal_len * inv_depth
    screen_u = near * in_camera[0]
    screen_v = near * in_camera[1]
    slope_u = screen_u * inv_depth
    slope_v = screen_v * inv_depth
    jac_u = [near * turned[0][k] - slope_u * turned[2][k] for k in range(3)]
    jac_v = [near * turned[1][k] - slope_v * turned[2][k] for k in range(3)]
    cov_uu = sum(jac_u[k] * jac_u[k] for k in range(3)) + dilation
    cov_uv = sum(jac_u[k] * jac_v[k] for k in range(3))
    cov_vv = sum(jac_v[k] * jac_v[k] for k in range(3)) + dilation
    inv_det = 1.0 / (cov_uu * cov_vv - cov_uv * cov_uv)
    toward = [center[i] + back[i] for i in range(3)]
    inv_len = 1.0 / jnp.sqrt(
        toward[0] * toward[0] + toward[1] * toward[1] + toward[2] * toward[2]
    )
    basis = sh_basis(toward[0] * inv_len, toward[1] * inv_len, toward[2] * inv_len)
    colors = [0.5 + sum(basis[k] * harmonics[3 * k + h] for k in range(16)) for h in range(3)]
    return [
        screen_u,
        screen_v,
        cov_vv * inv_det,
        -cov_uv * inv_det,
        cov_uu * inv_det,
    ] + colors


def log_opacity(logit):
    return jnp.minimum(logit, 0.0) - jnp.log1p(jnp.exp(-jnp.abs(logit)))


def pieces(value, count):
    out = []
    for _ in range(count - 1):
        top = value.astype(bf16).astype(f32)
        out.append(top)
        value = value - top
    out.append(value.astype(bf16).astype(f32))
    return out


def iota(shape, axis):
    return lax.broadcasted_iota(jnp.int32, shape, axis)


def order_kernel(requests_hbm, lists_hbm, out_ref, requests, lists, turned, sems):
    copies = [
        pltpu.make_async_copy(lists_hbm, lists.at[0:16], sems.at[0]),
        pltpu.make_async_copy(requests_hbm, requests, sems.at[1]),
    ]
    for copy in copies:
        copy.start()
    lists[16:128] = jnp.zeros((112, 512), jnp.int32)
    for copy in copies:
        copy.wait()
    turned[...] = lists[...].T
    group = iota((64, 128), 1) // 16
    entry = jnp.zeros((64, 128), jnp.int32)
    for j in range(8):
        piece = turned[pl.ds(j, 64, stride=8), :]
        if j:
            piece = pltpu.roll(piece, 16 * j, 1)
        entry = jnp.where(group == j, piece, entry)
    out_ref[...] = jnp.take_along_axis(requests[...], entry & 127, axis=1)


def camera_values(table_ref, view_ref):
    row = view_ref[0]
    return [jnp.full((8, 128), table_ref[i, row], f32) for i in range(8)]


def tile_frame(plan_ref, length_ref):
    lane_tile = iota((8, 128), 1) & 15
    center_u = jnp.zeros((8, 128), f32)
    center_v = jnp.zeros((8, 128), f32)
    length = jnp.zeros((8, 128), jnp.int32)
    for t in range(16):
        tile = plan_ref[0, t]
        down = tile // 120
        across = tile - down * 120
        at_u = (across * 16 + 8 - 960).astype(f32)
        at_v = (down * 16 + 8 - 540).astype(f32)
        center_u = jnp.where(lane_tile == t, at_u, center_u)
        center_v = jnp.where(lane_tile == t, at_v, center_v)
        length = jnp.where(lane_tile == t, length_ref[0, t], length)
    return center_u / 540.0, center_v / 540.0, length


def project_kernel(
    table_ref, view_ref, gauss_hbm, out_ref, spread, gauss, held, sems
):
    def fetch(i):
        column = pl.ds(pl.multiple_of(i * 1024, 1024), 1024)
        return pltpu.make_async_copy(gauss_hbm.at[:, column], gauss.at[:, column], sems.at[i])

    for i in range(8):
        fetch(i).start()
    view = view_values(camera_values(table_ref, view_ref))

    def step(i, carry):
        at = i * (8 * pitch)
        fetch(i).wait()
        for tile in range(8):
            column = pl.ds(pl.multiple_of(i * 1024 + tile * 128, 128), 128)
            row = pl.multiple_of(at + tile * pitch, 8)
            spread[pl.ds(row, 56), :] = gauss[0:56, column]
            spread[pl.ds(row + 56, 3), :] = gauss[56:59, column]
        params = [spread[pl.ds(at + p, 8, stride=pitch), :] for p in range(params_n)]
        shaped = shape_matrix(params[3:10])
        for k in range(9):
            spread[pl.ds(at + params_n + k, 8, stride=pitch), :] = shaped[k // 3][k % 3]
        out = project(params[0:3], shaped, params[11:], view)
        out = out[:5] + [log_opacity(params[10])] + out[5:]
        for f in range(feats):
            held[f, pl.ds(pl.multiple_of(i * 8, 8), 8), :] = out[f]
        return carry

    lax.fori_loop(0, 8, step, 0)
    for f in range(feats):
        for part, value in enumerate(pieces(held[f], 3 if f < 2 else 2)):
            row = (part * feats + f) * 32
            out_ref[row : row + 32, 0:128] = value[0:32].astype(bf16)
            out_ref[row : row + 32, 128:256] = value[32:64].astype(bf16)


def slot_hot(index):
    place = (index >> 12) * 128 + (index & 127)
    return (iota((256, index.shape[1]), 0) == place).astype(f32).astype(bf16)


def pick_rows(index_ref, table_ref, held, third):
    rows = feats * 32

    def step(pair, carry):
        index = jnp.concatenate(
            [index_ref[pl.ds(2 * pair, 1), :], index_ref[pl.ds(2 * pair + 1, 1), :]], axis=1
        )
        got = jnp.dot(table_ref[...], slot_hot(index), preferred_element_type=f32)
        level = (index >> 7) & 31
        keep = iota((32, 256), 0) == level
        for f in range(feats):
            value = got[32 * f : 32 * f + 32] + got[rows + 32 * f : rows + 32 * f + 32]
            if f < third:
                value += got[2 * rows + 32 * f : 2 * rows + 32 * f + 32]
            value = jnp.sum(jnp.where(keep, value, 0.0), axis=0, keepdims=True)
            held(f, 2 * pair, value[:, 0:128])
            held(f, 2 * pair + 1, value[:, 128:256])
        return carry

    lax.fori_loop(0, index_ref.shape[0] // 2, step, 0, unroll=pick_unroll)


def pick_kernel(index_ref, table_ref, out_ref, held):
    def keep(f, row, value):
        held[f, pl.ds(row, 1), :] = value

    pick_rows(index_ref, table_ref, keep, 2)
    for f in range(feats):
        out_ref[pl.ds(f, 64, stride=feats), :] = held[f]


def inverse_kernel(index_ref, out_ref, total):
    total[...] = jnp.zeros_like(total)

    def step(pair, carry):
        index = jnp.concatenate(
            [index_ref[pl.ds(2 * pair, 1), :], index_ref[pl.ds(2 * pair + 1, 1), :]], axis=1
        )
        keep = iota((32, 256), 0) == ((index >> 7) & 31)
        lane = iota((32, 256), 1)
        row = (2 * pair + (lane >> 7)).astype(f32)
        column = (lane & 127).astype(f32)
        both = jnp.concatenate([jnp.where(keep, row, 0.0), jnp.where(keep, column, 0.0)], axis=0)
        total[...] += lax.dot_general(
            both.astype(bf16),
            slot_hot(index),
            (((1,), (1,)), ((), ())),
            preferred_element_type=f32,
        )
        return carry

    lax.fori_loop(0, 32, step, 0, unroll=4)
    spot = (total[0:32] * 128.0 + total[32:64]).astype(jnp.int32)
    out_ref[0:32, :] = spot[:, 0:128]
    out_ref[32:64, :] = spot[:, 128:256]


def place_kernel(camera_ref, view_ref, index_ref, grad_ref, low_ref, high_ref, table):
    for f in range(feats):
        value = grad_ref[pl.ds(f, 64, stride=feats), :]
        for part, piece in enumerate(pieces(value, 2)):
            row = (part * feats + f) * 32
            table[row : row + 32, 0:128] = piece[0:32].astype(bf16)
            table[row : row + 32, 128:256] = piece[32:64].astype(bf16)
    lane = iota((8, 128), 1)
    camera = jnp.zeros((8, 128), f32)
    for i in range(8):
        camera = jnp.where(lane == i, camera_ref[i, view_ref[0]], camera)
    for half, out_ref in enumerate((low_ref, high_ref)):
        out_ref[feats * 32 :, :] = camera

        def keep(f, row, value, out_ref=out_ref):
            out_ref[pl.ds(f * 32 + row, 1), :] = value

        pick_rows(index_ref.at[32 * half : 32 * half + 32], table, keep, 0)


def pick(incoming, table):
    return call(
        pick_kernel,
        jax.ShapeDtypeStruct((64 * feats, 128), f32),
        (incoming, table),
        [vmem, vmem],
        [pltpu.VMEM((feats, 64, 128), f32)],
    )


def invert(incoming):
    return call(
        inverse_kernel,
        jax.ShapeDtypeStruct((64, 128), jnp.int32),
        (incoming,),
        [vmem],
        [pltpu.VMEM((64, 256), f32)],
    )


def place(camera_table, view_camera, inverse, returned):
    out = jax.ShapeDtypeStruct((half_rows, 128), f32)
    return call(
        place_kernel,
        (out, out),
        (camera_table, view_camera, inverse, returned),
        [smem, smem, vmem, vmem],
        [pltpu.VMEM((2 * feats * 32, 256), bf16)],
    )


def tile_colors(rows_ref, i):
    own_tile = iota((16, 256), 0) == (iota((16, 256), 1) & 15)
    high = []
    low = []
    for h in range(3):
        lines = [pl.ds((2 * i + own) * feats + 6 + h, 1) for own in range(2)]
        value = jnp.concatenate([rows_ref[line, :] for line in lines], axis=1)
        parts = pieces(jnp.where(own_tile, value, 0.0), 2)
        high.append(parts[0])
        low.append(parts[1])
    return jnp.concatenate(high + low, axis=0)


def render_kernel(
    plan_ref,
    length_ref,
    rows_ref,
    cot_ref,
    made_hbm,
    out_ref,
    weights,
    coef,
    alphas,
    shades,
    moments,
    tints,
    sems,
):
    store_rows = pltpu.make_async_copy(
        rows_ref, made_hbm.at[features_at : features_at + 64 * feats, 0:128], sems.at[32]
    )
    store_rows.start()
    lane_step = iota((8, 128), 1) >> 4
    center_u, center_v, length = tile_frame(plan_ref, length_ref)

    def feature(i, f):
        return rows_ref[pl.ds(i * (8 * feats) + f, 8, stride=feats), :]

    coef[...] = jnp.zeros_like(coef)

    def prepare(i, carry):
        off_u = (feature(i, 0) - center_u) * unit
        off_v = (feature(i, 1) - center_v) * unit
        quad_u = feature(i, 2) * (-0.5 * log2e / (unit * unit))
        quad_m = feature(i, 3) * (-log2e / (unit * unit))
        quad_v = feature(i, 4) * (-0.5 * log2e / (unit * unit))
        lead = quad_u * off_u + quad_m * off_v
        base = off_u * lead + quad_v * off_v * off_v + feature(i, 5) * log2e
        alive = (iota((8, 128), 0) + 8 * i) * 8 + lane_step < length
        values = [
            jnp.where(alive, base, -30000.0),
            jnp.where(alive, -(lead + quad_u * off_u), 0.0),
            jnp.where(alive, -(2.0 * quad_v * off_v + quad_m * off_u), 0.0),
            jnp.where(alive, quad_u, 0.0),
            jnp.where(alive, quad_m, 0.0),
            jnp.where(alive, quad_v, 0.0),
        ]
        for m, value in enumerate(values):
            coef[pl.ds(i * 64 + m, 8, stride=8), :] = value
        return carry

    lax.fori_loop(0, 8, prepare, 0)

    def monomials(shape):
        row = iota(shape, 0) & 7
        pixel = iota(shape, 1)
        at_x = ((pixel & 15) * 2 - 15).astype(f32)
        at_y = ((pixel >> 4) * 2 - 15).astype(f32)
        out = jnp.where(row == 0, 1.0, 0.0)
        out = jnp.where(row == 1, at_x, out)
        out = jnp.where(row == 2, at_y, out)
        out = jnp.where(row == 3, at_x * at_x, out)
        out = jnp.where(row == 4, at_x * at_y, out)
        return jnp.where(row == 5, at_y * at_y, out)

    terms = jnp.where(iota((32, 256), 0) < 24, monomials((32, 256)), 0.0).astype(bf16)
    moment_terms = monomials((16, 256)).astype(bf16)
    cot_parts = [pieces(cot_ref[h], 2) for h in range(3)]
    cot_high = jnp.concatenate([p[0] for p in cot_parts], axis=0).astype(bf16)
    cot_low = jnp.concatenate([p[1] for p in cot_parts], axis=0).astype(bf16)
    cot_both = jnp.concatenate([cot_high, cot_low], axis=0)
    cot_all = jnp.concatenate([cot_high, cot_high, cot_low], axis=0)
    same_tile = (iota((48, 256), 0) & 15) == (iota((48, 256), 1) & 15)
    across = (((1,), (1,)), ((), ()))
    along = (((0,), (0,)), ((), ()))

    def lay(i, carry):
        raw = jnp.concatenate(
            [
                coef[pl.ds(pl.multiple_of(i * 16, 8), 8), :],
                coef[pl.ds(pl.multiple_of(i * 16 + 8, 8), 8), :],
            ],
            axis=1,
        )
        block = jnp.concatenate(pieces(raw, 3) + [jnp.zeros((8, 256), f32)], axis=0)
        base = pl.multiple_of(i * 256, 256)
        power = lax.dot_general(
            block.astype(bf16), terms, along, preferred_element_type=f32
        )
        alphas[pl.ds(base, 256), :] = jnp.exp2(power)
        color = tile_colors(rows_ref, i)
        color = jnp.concatenate([color, color[0:48]], axis=0).astype(bf16)
        shades[pl.ds(base, 256), :] = lax.dot_general(
            color, cot_all, along, preferred_element_type=f32
        )
        return carry

    lax.fori_loop(0, 32, lay, 0, unroll=lay_unroll)

    def store(i):
        rows = pl.ds(pl.multiple_of(i * 256, 256), 256)
        return pltpu.make_async_copy(weights.at[rows], made_hbm.at[rows], sems.at[i])


    def forward(i, clear):
        base = pl.multiple_of(i * 256, 256)
        kept = []
        for k in range(16):
            weight = alphas[pl.ds(base + 16 * k, 16), :] * clear
            clear = clear - weight
            kept.append(weight)
        weight = jnp.concatenate(kept, axis=0)
        weights[pl.ds(base, 256), :] = weight
        store(i).start()
        top = weight.astype(bf16)
        low = (weight - top.astype(f32)).astype(bf16)
        both = lax.dot_general(cot_both, top, across, preferred_element_type=f32)
        tint = both[0:48] + both[48:96]
        tint += lax.dot_general(cot_high, low, across, preferred_element_type=f32)
        tint = jnp.where(same_tile, tint, 0.0)
        for h in range(3):
            value = jnp.sum(tint[16 * h : 16 * h + 16], axis=0, keepdims=True)
            for own in range(2):
                tints[h, pl.ds(2 * i + own, 1), :] = value[:, 128 * own : 128 * own + 128]
        return clear

    lax.fori_loop(0, 32, forward, jnp.ones((16, 256), f32), unroll=forward_unroll)

    def backward(step, behind):
        i = 31 - step
        base = pl.multiple_of(i * 256, 256)
        kept = [None] * 16
        for k in range(15, -1, -1):
            rows = pl.ds(base + 16 * k, 16)
            alpha = alphas[rows, :]
            shown = shades[rows, :]
            kept[k] = weights[rows, :] * (shown - behind)
            behind = (1.0 - alpha) * behind + alpha * shown
        slope = jnp.concatenate(kept, axis=0)
        top = slope.astype(bf16)
        low = (slope - top.astype(f32)).astype(bf16)
        moment = lax.dot_general(moment_terms, top, across, preferred_element_type=f32)
        moment += lax.dot_general(moment_terms, low, across, preferred_element_type=f32)
        for own in range(2):
            moments[pl.ds(pl.multiple_of(i * 16 + own * 8, 8), 8), :] = moment[
                0:8, 128 * own : 128 * own + 128
            ]
        return behind

    lax.fori_loop(0, 32, backward, jnp.zeros((16, 256), f32), unroll=backward_unroll)

    def finish(i, carry):
        off_u = (feature(i, 0) - center_u) * unit
        off_v = (feature(i, 1) - center_v) * unit
        m_one, m_x, m_y, m_xx, m_xy, m_yy = [
            moments[pl.ds(i * 64 + m, 8, stride=8), :] for m in range(6)
        ]
        n_x = m_x - off_u * m_one
        n_y = m_y - off_v * m_one
        n_xx = m_xx - off_u * (m_x + n_x)
        n_xy = m_xy - off_u * m_y - off_v * n_x
        n_yy = m_yy - off_v * (m_y + n_y)
        values = [
            (feature(i, 2) * n_x + feature(i, 3) * n_y) * (1.0 / unit),
            (feature(i, 3) * n_x + feature(i, 4) * n_y) * (1.0 / unit),
            n_xx * (-0.5 / (unit * unit)),
            n_xy * (-1.0 / (unit * unit)),
            n_yy * (-0.5 / (unit * unit)),
            m_one,
        ]
        for h in range(3):
            values.append(tints[h, pl.ds(pl.multiple_of(i * 8, 8), 8), :])
        for f, value in enumerate(values):
            out_ref[pl.ds(i * (8 * feats) + f, 8, stride=feats), :] = value
        return carry

    lax.fori_loop(0, 8, finish, 0)
    store_rows.wait()
    for i in range(32):
        store(i).wait()


def image_kernel(weights, rows_ref, image_ref):
    @pl.when(pl.program_id(0) == 0)
    def _():
        image_ref[...] = jnp.zeros_like(image_ref)

    for i in range(image_step):
        weight = weights[256 * i : 256 * i + 256, :]
        top = weight.astype(bf16)
        low = (weight - top.astype(f32)).astype(bf16)
        color = tile_colors(rows_ref, pl.program_id(0) * image_step + i).astype(bf16)
        both = jnp.dot(color, top, preferred_element_type=f32)
        image = both[0:48] + both[48:96]
        image += jnp.dot(color[0:48], low, preferred_element_type=f32)
        for h in range(3):
            image_ref[h] += image[16 * h : 16 * h + 16]


def render(tile_plan, tile_lengths, arrived, cots):
    shape = jax.ShapeDtypeStruct
    hbm = pl.BlockSpec(memory_space=pltpu.HBM)
    return call(
        render_kernel,
        (
            shape((features_at + 64 * feats, 256), f32),
            shape((64 * feats, 128), f32),
        ),
        (tile_plan, tile_lengths, arrived, cots),
        [smem, smem, vmem, vmem],
        [
            pltpu.VMEM((8192, 256), f32),
            pltpu.VMEM((512, 128), f32),
            pltpu.VMEM((8192, 256), f32),
            pltpu.VMEM((8192, 256), f32),
            pltpu.VMEM((512, 128), f32),
            pltpu.VMEM((3, 64, 128), f32),
            pltpu.SemaphoreType.DMA((33,)),
        ],
        52,
        (hbm, vmem),
    )


def compose(made):
    return pl.pallas_call(
        image_kernel,
        out_shape=jax.ShapeDtypeStruct((3, 16, 256), f32),
        grid=(32 // image_step,),
        in_specs=[
            pl.BlockSpec((256 * image_step, 256), lambda i: (i, 0)),
            pl.BlockSpec((64 * feats, 128), lambda i: (features_at // (64 * feats), 0)),
        ],
        out_specs=pl.BlockSpec((3, 16, 256), lambda i: (0, 0, 0)),
        compiler_params=pltpu.CompilerParams(vmem_limit_bytes=60 * 1024 * 1024),
    )(made, made)


def source_views(refs):
    sources = []
    for low, high in zip(refs[0::2], refs[1::2]):
        line = low[feats * 32 : feats * 32 + 8, :]
        camera = [jnp.broadcast_to(line[:, i : i + 1], (8, 128)) for i in range(8)]
        sources.append(((low, high), view_values(camera)))
    return sources


def view_gradient(sources, spread, step):
    at = step * (8 * pitch)
    first = step < 4

    def param(p):
        return spread[pl.ds(at + p, 8, stride=pitch), :]

    center = [param(p) for p in range(3)]
    shaped = [[param(params_n + 3 * j + k) for k in range(3)] for j in range(3)]
    harmonics = [param(p) for p in range(11, params_n)]
    total = None
    for (low, high), view in sources:
        lines = [pl.ds(32 * f + 8 * (step & 3), 8) for f in range(feats)]
        rows = [jnp.where(first, low[line, :], high[line, :]) for line in lines]

        def one(center, shaped, harmonics, view=view):
            return project(center, shaped, harmonics, view)

        _, back = jax.vjp(one, center, shaped, harmonics)
        d_center, d_shaped, d_harmonics = back(rows[:5] + rows[6:])
        part = d_center + sum(d_shaped, []) + [rows[5]] + d_harmonics
        total = part if total is None else [x + y for x, y in zip(total, part)]
    return total


def first_kernel(spread, low_ref, high_ref, out_ref):
    sources = source_views([low_ref, high_ref])

    def step(i, carry):
        rows = pl.ds(pl.multiple_of(i * 8, 8), 8)
        for p, value in enumerate(view_gradient(sources, spread, i)):
            out_ref[p, rows, :] = value
        return carry

    lax.fori_loop(0, 8, step, 0)


def middle_kernel(spread, left_low, left_high, right_low, right_high, sum_ref, out_ref):
    sources = source_views([left_low, left_high, right_low, right_high])

    def step(i, carry):
        rows = pl.ds(pl.multiple_of(i * 8, 8), 8)
        for p, value in enumerate(view_gradient(sources, spread, i)):
            out_ref[p, rows, :] = value + sum_ref[p, rows, :]
        return carry

    lax.fori_loop(0, 8, step, 0)


def last_kernel(spread, low_ref, high_ref, sum_ref, out_hbm, held, out_ref, sems):
    sources = source_views([low_ref, high_ref])

    def copy(i):
        column = pl.ds(pl.multiple_of(i * 1024, 1024), 1024)
        return pltpu.make_async_copy(out_ref.at[:, column], out_hbm.at[:, column], sems.at[i])

    def step(i, carry):
        rows = pl.ds(pl.multiple_of(i * 8, 8), 8)
        total = view_gradient(sources, spread, i)
        total = [value + sum_ref[p, rows, :] for p, value in enumerate(total)]
        params = [spread[pl.ds(i * (8 * pitch) + p, 8, stride=pitch), :] for p in range(3, 11)]
        _, back = jax.vjp(lambda *p: shape_matrix(p), *params[:7])
        d_shape = back([total[3 + 3 * j : 6 + 3 * j] for j in range(3)])
        d_logit = total[12] / (1.0 + jnp.exp(params[7]))
        for p, value in enumerate(total[0:3] + list(d_shape) + [d_logit] + total[13:]):
            held[pl.ds(p, 8, stride=pitch), :] = value
        for tile in range(8):
            column = pl.ds(pl.multiple_of(i * 1024 + tile * 128, 128), 128)
            row = tile * pitch
            out_ref[0:56, column] = held[row : row + 56, :]
            out_ref[56:59, column] = held[row + 56 : row + 59, :]
        copy(i).start()
        return carry

    lax.fori_loop(0, 8, step, 0)
    for i in range(8):
        copy(i).wait()


def call(kernel, out, args, specs, scratch, limit=8, out_specs=None):
    return pl.pallas_call(
        kernel,
        out_shape=out,
        in_specs=specs,
        out_specs=out_specs or jax.tree.map(lambda _: vmem, out),
        scratch_shapes=scratch,
        compiler_params=pltpu.CompilerParams(vmem_limit_bytes=limit * 1024 * 1024),
    )(*args)


def exchange(rows, width):
    parts = rows.reshape(owners, width, 1, 128)
    parts = lax.all_to_all(parts, "space", split_axis=0, concat_axis=0, tiled=True)
    return parts.reshape(owners * width, 128)


def per_device(
    gaussians, camera_table, view_camera, tile_plan, requests, tile_lists, tile_lengths, pixel_grad
):
    shape = jax.ShapeDtypeStruct
    ordered = call(
        order_kernel,
        shape((64, 128), jnp.int32),
        (requests[0, 0], tile_lists[0]),
        [pl.BlockSpec(memory_space=pltpu.HBM)] * 2,
        [
            pltpu.VMEM((64, 128), jnp.int32),
            pltpu.VMEM((128, 512), jnp.int32),
            pltpu.VMEM((512, 128), jnp.int32),
            pltpu.SemaphoreType.DMA((2,)),
        ],
        60,
    )
    incoming = exchange(ordered, 1)
    table, spread = call(
        project_kernel,
        (
            shape(((2 * feats + 2) * 32, 256), bf16),
            shape((64 * pitch, 128), f32),
        ),
        (camera_table.T, view_camera, gaussians),
        [smem, smem, pl.BlockSpec(memory_space=pltpu.HBM)],
        [
            pltpu.VMEM((params_n, slots), f32),
            pltpu.VMEM((feats, 64, 128), f32),
            pltpu.SemaphoreType.DMA((8,)),
        ],
        16,
    )
    picked = pick(incoming, table)
    arrived = exchange(picked, feats)
    inverse = invert(incoming)
    made, row_grad = render(
        tile_plan, tile_lengths, arrived, jnp.transpose(pixel_grad[0], (1, 0, 2))
    )
    returned = exchange(row_grad, feats)
    image = compose(made)
    returned, image = lax.optimization_barrier((returned, image))
    low, high = place(camera_table.T, view_camera, inverse, returned)
    ahead = [(i, (i + 1) % 4) for i in range(4)]
    behind = [(i, (i - 1) % 4) for i in range(4)]
    left_low = lax.ppermute(low, "view", ahead)
    right_high = lax.ppermute(high, "view", behind)
    left_high = lax.ppermute(high, "view", ahead)
    right_low = lax.ppermute(low, "view", behind)
    part = shape((61, 64, 128), f32)
    total = call(first_kernel, part, (spread, low, high), [vmem] * 3, [], 12)
    left_low, right_high, total = lax.optimization_barrier((left_low, right_high, total))
    far_low = lax.ppermute(left_low, "view", ahead)
    far_high = lax.ppermute(right_high, "view", behind)
    total = call(
        middle_kernel,
        part,
        (spread, left_low, left_high, right_low, right_high, total),
        [vmem] * 6,
        [],
        16,
    )
    total = call(
        last_kernel,
        shape((params_n, slots), f32),
        (spread, far_low, far_high, total),
        [vmem] * 4,
        [
            pltpu.VMEM((8 * pitch, 128), f32),
            pltpu.VMEM((params_n, slots), f32),
            pltpu.SemaphoreType.DMA((8,)),
        ],
        16,
        pl.BlockSpec(memory_space=pltpu.HBM),
    )
    return (jnp.transpose(image, (1, 0, 2))[None], total)


def solution(mesh):
    placed = (
        P(None, "space"),
        P(),
        P("view"),
        P("view", "space"),
        P("view", "space", None, None),
        P("view", "space", None),
        P("view", "space"),
        P("view", "space", None, None),
    )
    return jax.shard_map(
        per_device,
        mesh=mesh,
        in_specs=placed,
        out_specs=(P("view", "space", None, None), P(None, "space")),
        check_vma=False,
    )
```
